32 devices in a mesh: section: 2 (over y), expert: 16 (over z, x, core).
Axes of the slice: x: 2, y: 2, z: 4, core: 2. Of those that a mesh axis runs over, the one named last changes fastest.
Arguments:
- embedded: bfloat16 [2048, 3584], P('expert'), may hold values from -6 to 6
- forward_held: bfloat16 [2, 2048, 3584], P('section', 'expert'), may hold values from -6 to 6
- forward_route: int32 [2, 2048, 1], P('section', 'expert'), may hold values from 0 to 3; in each aligned block of 128 rows (0 to 127, 128 to 255, ..., all dimensions but the last counted through in order) at most 48 rows name the same one
- forward_weight: float32 [2, 2048], P('section', 'expert'), may hold values from 0.2 to 1
- loss_cotangent: bfloat16 [2048, 3584], P('expert'), may hold values from -6 to 6
- backward_held: bfloat16 [2, 2048, 3584], P('section', 'expert'), may hold values from -6 to 6
- backward_route: int32 [2, 2048, 1], P('section', 'expert'), may hold values from 0 to 3; in each aligned block of 128 rows (0 to 127, 128 to 255, ..., all dimensions but the last counted through in order) at most 48 rows name the same one
- backward_weight: float32 [2, 2048], P('section', 'expert'), may hold values from 0.2 to 1
- saved_gate: bfloat16 [2, 768, 4096], P('section', None, 'expert'), may hold values from -6 to 6
- saved_up: bfloat16 [2, 768, 4096], P('section', None, 'expert'), may hold values from -6 to 6
- gate_weight: bfloat16 [2, 3584, 4096], P('section', None, 'expert'), may hold values from -0.09375 to 0.09375
- up_weight: bfloat16 [2, 3584, 4096], P('section', None, 'expert'), may hold values from -0.09375 to 0.09375
- down_weight: bfloat16 [2, 4096, 3584], P('section', 'expert'), may hold values from -0.1875 to 0.1875
- steering: float32 [2, 3584], P('section'), may hold values from -6 to 6
Outputs:
- forward_out: bfloat16 [2, 2048, 3584], P('section', 'expert')
- forward_coefficient: float32 [2, 2048], P('section', 'expert')
- backward_out: bfloat16 [2, 2048, 3584], P('section', 'expert')
The draws below stay inside these ranges and needn't reach their ends.
Inputs may be any that keep to these rules, and one draw needn't show every extreme that they name: `forward_route`: in each aligned block of 128 tokens of a layer (the tokens of one device) no expert is chosen more than 48 times, and some expert is chosen exactly 48 times in some block. `backward_route`: in each aligned block of 128 tokens of a layer (the tokens of one device) no expert is chosen more than 48 times, and some expert is chosen exactly 48 times in some block.
All inputs are finite; a program needn't handle non-finite values.
Results may differ from the reference program's by a relative error of at most 0.0058.
Values may be sent and summed in bfloat16 or wider, within the bound.
No kernel may reach another device: no remote copies, remote signals or barrier semaphores. Data moves between devices by JAX's collectives and lax.ppermute only.
A program may use at most 64 MiB of HBM per device.

```python
import math
import jax
import jax.numpy as jnp
import numpy as np
from jax import lax

D = 3584
H = 1024
HDEV = 256
TOK_DEV = 128
EXPERTS = 4
CAP = 48
MB_TOK = 2048
N_SECTION = 2
N_EXPERT = 16


def shard_levels(stream_key, dims, cuts, smallest, top_value):
    factor_of, own = 1.0, jax.random.fold_in(stream_key, 6)
    for axis_at, parts in cuts:
        draws = jnp.exp(jax.random.uniform(jax.random.fold_in(own, axis_at), (parts,), jnp.float32, smallest / len(cuts), top_value / len(cuts)))
        factor_of = factor_of * jnp.repeat(draws, dims[axis_at] // parts).reshape([-1 if axis == axis_at else 1 for axis in range(len(dims))])
    return factor_of


def shared_out(stream_key, own, number, rows, count, top, bound, skew):
    ranking = jax.random.permutation(stream_key, count)
    crowded, usual = portions_of(count, rows * top, bound, skew, True), portions_of(count, rows * top, bound, skew, False)
    places = jnp.arange(count)

    def named(tallies, rotation):
        used = int((tallies > 0).sum())
        fixed = max(1, used // 4)
        shifted = fixed + (places - fixed + rotation * (used - fixed)) % max(1, count - fixed)
        return jnp.zeros((count,), jnp.int32).at[ranking[jnp.where(places < fixed, places, shifted)]].set(jnp.asarray(tallies, jnp.int32))

    tallies = jnp.where(number % 4 == 0, named(crowded, number // 4), named(usual, number - number // 4 - 1))
    mixed = jax.random.permutation(jax.random.fold_in(own, 3), count)
    donor, taker = mixed[0:count // 2 * 2:2], mixed[1:count // 2 * 2:2]
    slack = jnp.minimum(tallies[donor] - 1, bound - tallies[taker]) // 2
    slack = jnp.where((donor == ranking[0]) | (taker == ranking[0]) | (tallies[taker] == 0), 0, jnp.maximum(slack, 0))
    shifted = jax.random.randint(jax.random.fold_in(own, 4), (count // 2,), 0, 1 << 20) % (slack + 1)
    tallies = tallies.at[donor].add(-shifted).at[taker].add(shifted)
    items = jnp.searchsorted(jnp.cumsum(tallies), jnp.arange(rows * top), side="right").astype(jnp.int32)
    table = items.reshape(top, rows).T
    table = table[jax.random.permutation(jax.random.fold_in(own, 1), rows)]
    rotation = jax.random.randint(jax.random.fold_in(own, 2), (rows, 1), 0, top)
    return jnp.take_along_axis(table, (jnp.arange(top)[None, :] + rotation) % top, axis=1)


def portions_of(count, total, bound, slope, full):
    portions = [(1 << 20) // math.isqrt(standing ** slope) + 1 for standing in range(1, count + 1)]
    largest = bound if full else min(bound, max(-(-total // count), total * portions[0] // sum(portions)))
    least = 1 if total - largest >= count - 1 else 0
    given, spare = [largest] + [least] * (count - 1), total - largest - least * (count - 1)
    while spare > 0:
        free = [i for i in range(1, count) if given[i] < largest] or [i for i in range(1, count) if given[i] < bound]
        whole, left = sum([portions[i] for i in free]), spare
        for i in free:
            addition = min(bound - given[i], max(1, left * portions[i] // whole), spare)
            given[i] = given[i] + addition
            spare = spare - addition
    return np.array(given)


def scatter_about(own_key, shape, width, most, shards=(), kind=jnp.bfloat16):
    result = width * jax.random.normal(own_key, shape, jnp.float32)
    if shards:
        result = result * shard_levels(own_key, shape, shards, -0.22, 0.18)
    return jnp.clip(result, -most, most).astype(kind)


def setup_inputs(seed: int = 0) -> dict:
    arg_keys = jax.random.split(jax.random.key(seed), 15)
    embedded = scatter_about(arg_keys[0], (MB_TOK, D), 1.0, 6.0, ((0, 16),))
    forward_held = scatter_about(arg_keys[1], (N_SECTION, MB_TOK, D), 1.0, 6.0, ((0, 2), (1, 16)))
    forward_route_keys = jax.random.split(jax.random.fold_in(arg_keys[2], 1), N_SECTION * MB_TOK // TOK_DEV)
    forward_route_turns = jax.random.permutation(jax.random.fold_in(arg_keys[2], 3), N_SECTION * MB_TOK // TOK_DEV)
    forward_route = jax.vmap(lambda own, number: shared_out(jax.random.fold_in(arg_keys[2], 2), own, number, TOK_DEV, EXPERTS, 1, CAP, 2))(forward_route_keys, forward_route_turns).reshape((N_SECTION, MB_TOK, 1))
    forward_weight = jnp.clip(0.2 + 0.8 * jax.random.uniform(arg_keys[3], (N_SECTION, MB_TOK), jnp.float32) ** shard_levels(arg_keys[3], (N_SECTION, MB_TOK), ((0, 2), (1, 16)), -0.2, 0.2), 0.2, 1.0)
    loss_cotangent = scatter_about(arg_keys[4], (MB_TOK, D), 1.0, 6.0, ((0, 16),))
    backward_held = scatter_about(arg_keys[5], (N_SECTION, MB_TOK, D), 1.0, 6.0, ((0, 2), (1, 16)))
    backward_route_keys = jax.random.split(jax.random.fold_in(arg_keys[6], 1), N_SECTION * MB_TOK // TOK_DEV)
    backward_route_turns = jax.random.permutation(jax.random.fold_in(arg_keys[6], 3), N_SECTION * MB_TOK // TOK_DEV)
    backward_route = jax.vmap(lambda own, number: shared_out(jax.random.fold_in(arg_keys[6], 2), own, number, TOK_DEV, EXPERTS, 1, CAP, 2))(backward_route_keys, backward_route_turns).reshape((N_SECTION, MB_TOK, 1))
    backward_weight = jnp.clip(0.2 + 0.8 * jax.random.uniform(arg_keys[7], (N_SECTION, MB_TOK), jnp.float32) ** shard_levels(arg_keys[7], (N_SECTION, MB_TOK), ((0, 2), (1, 16)), -0.2, 0.2), 0.2, 1.0)
    saved_gate = scatter_about(arg_keys[8], (N_SECTION, N_EXPERT * CAP, EXPERTS * H), 1.0, 6.0, ((0, 2), (2, 16)))
    saved_up = scatter_about(arg_keys[9], (N_SECTION, N_EXPERT * CAP, EXPERTS * H), 1.0, 6.0, ((0, 2), (2, 16)))
    gate_weight = scatter_about(arg_keys[10], (N_SECTION, D, EXPERTS * H), D ** -0.5, 0.09375, ((0, 2), (2, 16)))
    up_weight = scatter_about(arg_keys[11], (N_SECTION, D, EXPERTS * H), D ** -0.5, 0.09375, ((0, 2), (2, 16)))
    down_weight = scatter_about(arg_keys[12], (N_SECTION, EXPERTS * H, D), H ** -0.5, 0.1875, ((0, 2), (1, 16)))
    steering = scatter_about(arg_keys[13], (N_SECTION, D), 1.0, 6.0, ((0, 2),), jnp.float32)
    return dict(embedded=embedded, forward_held=forward_held, forward_route=forward_route, forward_weight=forward_weight, loss_cotangent=loss_cotangent, backward_held=backward_held, backward_route=backward_route, backward_weight=backward_weight, saved_gate=saved_gate, saved_up=saved_up, gate_weight=gate_weight, up_weight=up_weight, down_weight=down_weight, steering=steering)


def placement_rows(route_section):
    expert_ids = route_section[:, 0].astype(jnp.int32)
    blocked = expert_ids.reshape(N_EXPERT, TOK_DEV)
    onehot = (blocked[:, :, None] == jnp.arange(EXPERTS, dtype=jnp.int32)[None, None, :]).astype(jnp.int32)
    earlier = jnp.cumsum(onehot, axis=1) - onehot
    position = lax.optimization_barrier(jnp.sum(earlier * onehot, axis=2))
    row_index = jnp.arange(N_EXPERT, dtype=jnp.int32)[:, None] * CAP + position
    return (expert_ids, row_index.reshape(MB_TOK).astype(jnp.int32))

def layout_of(expert_ids, row_index):
    layout = jnp.full((EXPERTS, N_EXPERT * CAP), MB_TOK, jnp.int32)
    return layout.at[expert_ids, row_index].set(jnp.arange(MB_TOK, dtype=jnp.int32))

def forward_expert(slot_rows, gate_cols, up_cols, down_rows):
    summed = jnp.zeros((slot_rows.shape[0], D), jnp.float32)
    for holder in range(H // HDEV):
        first_col = holder * HDEV
        gate_pre = jnp.dot(slot_rows, gate_cols[:, first_col:first_col + HDEV], preferred_element_type=jnp.float32)
        up_pre = jnp.dot(slot_rows, up_cols[:, first_col:first_col + HDEV], preferred_element_type=jnp.float32)
        hidden = (jax.nn.silu(gate_pre) * up_pre).astype(jnp.bfloat16)
        partial_out = jnp.dot(hidden, down_rows[first_col:first_col + HDEV], preferred_element_type=jnp.float32).astype(jnp.bfloat16)
        summed = summed + partial_out.astype(jnp.float32)
    return summed.astype(jnp.bfloat16)

def backward_expert(slot_rows, gate_saved, up_saved, gate_cols, up_cols, down_rows):
    contract = (((1,), (1,)), ((), ()))
    summed = jnp.zeros((slot_rows.shape[0], D), jnp.float32)
    for holder in range(H // HDEV):
        first_col = holder * HDEV
        grad_hidden = lax.dot_general(slot_rows, down_rows[first_col:first_col + HDEV], contract, preferred_element_type=jnp.float32)
        gate_pre = gate_saved[:, first_col:first_col + HDEV].astype(jnp.float32)
        up_pre = up_saved[:, first_col:first_col + HDEV].astype(jnp.float32)
        sigmoid_gate = jax.nn.sigmoid(gate_pre)
        grad_gate = (grad_hidden * up_pre * sigmoid_gate * (1.0 + gate_pre * (1.0 - sigmoid_gate))).astype(jnp.bfloat16)
        grad_up = (grad_hidden * gate_pre * sigmoid_gate).astype(jnp.bfloat16)
        grad_part = lax.dot_general(grad_gate, gate_cols[:, first_col:first_col + HDEV], contract, preferred_element_type=jnp.float32)
        grad_part = grad_part + lax.dot_general(grad_up, up_cols[:, first_col:first_col + HDEV], contract, preferred_element_type=jnp.float32)
        summed = summed + grad_part.astype(jnp.bfloat16).astype(jnp.float32)
    return summed.astype(jnp.bfloat16)

def one_section(operands):
    forward_in, backward_in, forward_route, forward_weight, backward_route, backward_weight, gate_store, up_store, gate_mat, up_mat, down_mat, steer_vec = operands
    unit_dir = steer_vec / jnp.sqrt(jnp.sum(steer_vec * steer_vec) + 1e-06)
    expert_ids, row_index = placement_rows(forward_route)
    layout = layout_of(expert_ids, row_index)
    padded = jnp.concatenate([forward_in, jnp.zeros((1, D), forward_in.dtype)], axis=0)
    forward_slots = padded[layout]

    def expert_forward(packed):
        expert_index, slot_rows = packed
        gate_cols = lax.dynamic_slice_in_dim(gate_mat, expert_index * H, H, 1)
        up_cols = lax.dynamic_slice_in_dim(up_mat, expert_index * H, H, 1)
        down_rows = lax.dynamic_slice_in_dim(down_mat, expert_index * H, H, 0)
        return forward_expert(slot_rows, gate_cols, up_cols, down_rows)
    forward_outs = lax.map(expert_forward, (jnp.arange(EXPERTS, dtype=jnp.int32), forward_slots))
    picked = forward_outs[expert_ids, row_index]
    mixed_rows = forward_weight[:, None] * picked.astype(jnp.float32)
    coefficient = lax.optimization_barrier(jnp.sum(mixed_rows * unit_dir[None, :], axis=1))
    forward_out = (forward_in.astype(jnp.float32) + mixed_rows - coefficient[:, None] * unit_dir[None, :]).astype(jnp.bfloat16)
    backward_dy = backward_in.astype(jnp.float32)
    along_dir = lax.optimization_barrier(jnp.sum(backward_dy * unit_dir[None, :], axis=1))
    sent_rows = (backward_weight[:, None] * (backward_dy - along_dir[:, None] * unit_dir[None, :])).astype(jnp.bfloat16)
    backward_ids, backward_index = placement_rows(backward_route)
    backward_layout = layout_of(backward_ids, backward_index)
    padded_sent = jnp.concatenate([sent_rows, jnp.zeros((1, D), sent_rows.dtype)], axis=0)
    backward_slots = padded_sent[backward_layout]

    def expert_backward(packed):
        expert_index, slot_rows = packed
        gate_cols = lax.dynamic_slice_in_dim(gate_mat, expert_index * H, H, 1)
        up_cols = lax.dynamic_slice_in_dim(up_mat, expert_index * H, H, 1)
        down_rows = lax.dynamic_slice_in_dim(down_mat, expert_index * H, H, 0)
        gate_saved = lax.dynamic_slice_in_dim(gate_store, expert_index * H, H, 1)
        up_saved = lax.dynamic_slice_in_dim(up_store, expert_index * H, H, 1)
        return backward_expert(slot_rows, gate_saved, up_saved, gate_cols, up_cols, down_rows)
    backward_outs = lax.map(expert_backward, (jnp.arange(EXPERTS, dtype=jnp.int32), backward_slots))
    returned = backward_outs[backward_ids, backward_index]
    backward_out = (backward_dy + returned.astype(jnp.float32)).astype(jnp.bfloat16)
    return (forward_out, coefficient, backward_out)

def reference(embedded, forward_held, forward_route, forward_weight, loss_cotangent, backward_held, backward_route, backward_weight, saved_gate, saved_up, gate_weight, up_weight, down_weight, steering):
    forward_inputs = jnp.concatenate([embedded[None], forward_held[:-1]], axis=0)
    backward_inputs = jnp.concatenate([backward_held[1:], loss_cotangent[None]], axis=0)
    results = lax.map(one_section, (forward_inputs, backward_inputs, forward_route, forward_weight, backward_route, backward_weight, saved_gate, saved_up, gate_weight, up_weight, down_weight, steering))
    return (results[0], results[1], results[2])
```

```python
import jax
import jax.numpy as jnp
from jax import lax
from jax.sharding import PartitionSpec as P

H = 1024
CORES = 2
BF16 = jnp.bfloat16
F32 = jnp.float32
ROWS_BY_ROWS = (((1,), (1,)), ((), ()))
COLS_BY_COLS = (((0,), (0,)), ((), ()))


def shifted(value, axis, by):
    devices = lax.axis_size(axis)
    pairs = [(i, i + by) for i in range(devices) if 0 <= i + by < devices]
    return lax.ppermute(value, axis, pairs)


def dispatch_layout(expert_ids, first_expert, expert_count, capacity):
    onehot = (expert_ids[:, None] == jnp.arange(expert_count, dtype=jnp.int32)[None, :]).astype(jnp.int32)
    earlier = jnp.cumsum(onehot, axis=0) - onehot
    position = jnp.sum(earlier * onehot, axis=1)
    target = lax.rem(expert_ids - first_expert + expert_count, expert_count) * capacity + position
    slots = jnp.arange(expert_count * capacity, dtype=jnp.int32)
    return (slots[:, None] == target[None, :]).astype(BF16)


def body(
    embedded,
    forward_held,
    forward_route,
    forward_weight,
    loss_cotangent,
    backward_held,
    backward_route,
    backward_weight,
    saved_gate,
    saved_up,
    gate_weight,
    up_weight,
    down_weight,
    steering,
):
    section_count = lax.axis_size("section")
    section_index = lax.axis_index("section")
    device_count = lax.axis_size("expert")
    device_index = lax.axis_index("expert")
    local_hidden = gate_weight.shape[2]
    holders = H // local_hidden
    experts = device_count // holders
    chips = holders // CORES
    capacity = saved_gate.shape[1] // device_count
    plane = device_index // holders
    chip = lax.rem(device_index, holders) // CORES
    core = lax.rem(device_index, CORES)

    def to_plane(value, by):
        pairs = [(i, (i + by * holders) % device_count) for i in range(device_count)]
        return lax.ppermute(value, "expert", pairs)

    def to_chip(value, by):
        pairs = [(i, i // holders * holders + (i + by * CORES) % holders) for i in range(device_count)]
        return lax.ppermute(value, "expert", pairs)

    def to_core(value):
        return lax.ppermute(value, "expert", [(i, i ^ 1) for i in range(device_count)])

    arriving = shifted(forward_held, "section", 1)[0]
    returning = shifted(backward_held, "section", -1)[0]
    forward_in = jnp.where(section_index == 0, embedded, arriving)
    backward_in = jnp.where(section_index == section_count - 1, loss_cotangent, returning)

    gate, up, down = gate_weight[0], up_weight[0], down_weight[0]
    gate_chip = jnp.concatenate([gate, to_core(gate)], axis=1)
    up_chip = jnp.concatenate([up, to_core(up)], axis=1)
    down_of = [down] + [to_chip(down, -s) for s in range(1, chips)]
    down_chips = [jnp.concatenate([d, to_core(d)], axis=0) for d in down_of]

    sources = (
        lax.rem(plane - jnp.arange(experts, dtype=jnp.int32) + experts, experts)[None, :] * holders
        + lax.rem(chip + jnp.arange(chips, dtype=jnp.int32), chips)[:, None] * CORES
    ).reshape(-1)

    def rows_of(core_index):
        wanted = ((sources + core_index)[:, None] * capacity + jnp.arange(capacity, dtype=jnp.int32)[None, :]).reshape(-1)
        return (wanted[:, None] == jnp.arange(saved_gate.shape[1], dtype=jnp.int32)[None, :]).astype(BF16)

    saved = jnp.concatenate([saved_gate[0], saved_up[0]], axis=1)
    saved_kept = jnp.dot(rows_of(core), saved, preferred_element_type=F32).astype(BF16)
    saved_got = to_core(jnp.dot(rows_of(1 - core), saved, preferred_element_type=F32).astype(BF16))
    gate_saved = jnp.concatenate([saved_kept[:, :local_hidden], saved_got[:, :local_hidden]], axis=1)
    up_saved = jnp.concatenate([saved_kept[:, local_hidden:], saved_got[:, local_hidden:]], axis=1)

    direction = steering[0]
    unit_dir = direction / jnp.sqrt(jnp.sum(direction * direction) + 1e-06)

    def dispatched(layout, tokens):
        chosen = jnp.dot(layout, tokens, preferred_element_type=F32).astype(BF16)
        blocks = [chosen[k * capacity : (k + 1) * capacity] for k in range(experts)]
        return [blocks[0]] + [to_plane(blocks[k], k) for k in range(1, experts)]

    def returned(blocks):
        back = [blocks[0]] + [to_plane(blocks[k], -k) for k in range(1, experts)]
        return jnp.concatenate(back, axis=0)

    def split(rows):
        return [rows[k * capacity : (k + 1) * capacity] for k in range(experts)]

    forward_layout = dispatch_layout(forward_route[0, :, 0], plane, experts, capacity)
    forward_blocks = dispatched(forward_layout, forward_in)
    backward_dy = backward_in.astype(F32)
    along_dir = jnp.sum(backward_dy * unit_dir[None, :], axis=1)
    sent_rows = (backward_weight[0][:, None] * (backward_dy - along_dir[:, None] * unit_dir[None, :])).astype(BF16)
    backward_layout = dispatch_layout(backward_route[0, :, 0], plane, experts, capacity)
    backward_blocks = dispatched(backward_layout, sent_rows)

    def hidden_of(rows):
        gate_pre = jnp.dot(rows, gate_chip, preferred_element_type=F32)
        up_pre = jnp.dot(rows, up_chip, preferred_element_type=F32)
        return (jax.nn.silu(gate_pre) * up_pre).astype(BF16)

    forward_rows = jnp.concatenate(forward_blocks, axis=0)
    hidden = [hidden_of(forward_rows)]
    for s in range(1, chips):
        across = jnp.concatenate([to_chip(block, s) for block in forward_blocks], axis=0)
        hidden.append(to_chip(hidden_of(across), -s))
    forward_part = sum(jnp.dot(hidden[s], down_chips[s], preferred_element_type=F32) for s in range(chips))
    forward_back = returned(split(forward_part.astype(BF16)))

    backward_rows = jnp.concatenate(backward_blocks, axis=0)
    grad_hidden = []
    for s in range(chips):
        grads = lax.dot_general(backward_rows, down_chips[s], ROWS_BY_ROWS, preferred_element_type=F32)
        grad_hidden.append(grads if s == 0 else to_chip(grads.astype(BF16), s).astype(F32))
    row_count = experts * capacity
    parts = []
    for s in range(chips):
        at = (chips - s) % chips
        gate_pre = gate_saved[at * row_count : (at + 1) * row_count].astype(F32)
        up_pre = up_saved[at * row_count : (at + 1) * row_count].astype(F32)
        sigmoid_gate = jax.nn.sigmoid(gate_pre)
        grad_gate = (grad_hidden[s] * up_pre * sigmoid_gate * (1.0 + gate_pre * (1.0 - sigmoid_gate))).astype(BF16)
        grad_up = (grad_hidden[s] * gate_pre * sigmoid_gate).astype(BF16)
        part = lax.dot_general(grad_gate, gate_chip, ROWS_BY_ROWS, preferred_element_type=F32)
        part = part + lax.dot_general(grad_up, up_chip, ROWS_BY_ROWS, preferred_element_type=F32)
        parts.append(part)
    mine = split(parts[0])
    for s in range(1, chips):
        got = [to_chip(block, -s) for block in split(parts[s].astype(BF16))]
        mine = [a + b.astype(F32) for a, b in zip(mine, got)]
    backward_back = returned([block.astype(BF16) for block in mine])

    picked = lax.dot_general(forward_layout, forward_back, COLS_BY_COLS, preferred_element_type=F32)
    mixed_rows = forward_weight[0][:, None] * picked
    coefficient = jnp.sum(mixed_rows * unit_dir[None, :], axis=1)
    forward_out = (forward_in.astype(F32) + mixed_rows - coefficient[:, None] * unit_dir[None, :]).astype(BF16)
    grad_rows = lax.dot_general(backward_layout, backward_back, COLS_BY_COLS, preferred_element_type=F32)
    backward_out = (backward_dy + grad_rows).astype(BF16)
    return (forward_out[None], coefficient[None], backward_out[None])


def solution(mesh):
    in_specs = (
        P("expert", None),
        P("section", "expert", None),
        P("section", "expert", None),
        P("section", "expert"),
        P("expert", None),
        P("section", "expert", None),
        P("section", "expert", None),
        P("section", "expert"),
        P("section", None, "expert"),
        P("section", None, "expert"),
        P("section", None, "expert"),
        P("section", None, "expert"),
        P("section", "expert", None),
        P("section", None),
    )
    out_specs = (P("section", "expert", None), P("section", "expert"), P("section", "expert", None))
    return jax.shard_map(body, mesh=mesh, in_specs=in_specs, out_specs=out_specs, check_vma=False)
```

```python
import functools

import jax
import jax.numpy as jnp
from jax import lax
from jax.experimental import pallas as pl
from jax.experimental.pallas import tpu as pltpu
from jax.sharding import PartitionSpec as P

H = 1024
CORES = 2
EARLY = (2,)
PARTS = 1
OPT = {'split_rows': True, 'pack': False, 'z_depth': 2, 'x_depth': 2, 'm_core': True, 'rows_got': False, 'rows_d1': False, 'rows_core': True, 'x_wd': False, 'd3_after': 1, 'one_group': False, 'gh_after': 0, 'mine_first': False, 'theirs_after': 0, 'wd_first': False, 'rs_order': [2, 1, 3, 0], 'h2_after': 0, 'limit_add': 24, 'limit_mm': 16, 'limit_rows': 24, 'limit_first': 56, 'br_dep': False, 'cost': {'grad_rows': 10000000000, 'add_rows': 2000000000, 'forward_end': 50000000000}}
COST = 5000000000
BF16 = jnp.bfloat16
F32 = jnp.float32
COLS = 896
ROWS_BY_ROWS = (((1,), (1,)), ((), ()))
SMEM = pl.BlockSpec(memory_space=pltpu.SMEM)
VMEM = pl.BlockSpec(memory_space=pltpu.VMEM)


def after(value, *deps):
    return lax.optimization_barrier((value, *deps))[0] if deps else value


def dot(a, b):
    return jnp.dot(a, b, preferred_element_type=F32)


def dot_rows(a, b):
    return lax.dot_general(a, b, ROWS_BY_ROWS, preferred_element_type=F32)


def shape(rows, cols, dtype=BF16):
    return jax.ShapeDtypeStruct((rows, cols), dtype)


def shifted(value, axis, by):
    devices = lax.axis_size(axis)
    pairs = [(i, i + by) for i in range(devices) if 0 <= i + by < devices]
    return lax.ppermute(value, axis, pairs)


def call(kernel, name, outs, args, grid=None, in_specs=None, out_specs=None, scratch=(), limit=24):
    extra = {} if grid is None else {"grid": grid}
    return pl.pallas_call(
        kernel,
        out_shape=outs,
        in_specs=in_specs,
        out_specs=out_specs if out_specs is not None else [VMEM] * len(outs),
        scratch_shapes=list(scratch),
        name=name,
        cost_estimate=pl.CostEstimate(flops=OPT["cost"].get(name, COST), bytes_accessed=100000, transcendentals=0),
        compiler_params=pltpu.CompilerParams(vmem_limit_bytes=limit << 20),
        **extra,
    )(*args)


def stacked(values):
    if values[0].shape[0] % 16 == 0:
        return jnp.concatenate(values, axis=0)
    return jnp.concatenate([value.astype(F32) for value in values], axis=0).astype(BF16)


def slot_of(ids, plane, experts, capacity, axis):
    tokens = ids.shape[axis]
    wide = (tokens, 128) if axis == 0 else (max(8, experts), tokens)
    chosen = jnp.where(ids == lax.broadcasted_iota(jnp.int32, wide, 1 - axis), 1.0, 0.0)
    row = lax.broadcasted_iota(jnp.int32, (tokens, tokens), 0)
    col = lax.broadcasted_iota(jnp.int32, (tokens, tokens), 1)
    if axis == 0:
        earlier = dot(jnp.where(col < row, 1.0, 0.0).astype(BF16), chosen.astype(BF16))
    else:
        earlier = dot(chosen.astype(BF16), jnp.where(row < col, 1.0, 0.0).astype(BF16))
    position = jnp.sum(chosen * earlier, axis=1 - axis, keepdims=True).astype(jnp.int32)
    ahead = ids - plane
    return jnp.where(ahead < 0, ahead + experts, ahead) * capacity + position


def slots_by_tokens(ids_row, plane, experts, capacity):
    wide = (experts * capacity, ids_row.shape[1])
    slot = slot_of(ids_row, plane, experts, capacity, 1)
    return jnp.where(lax.broadcasted_iota(jnp.int32, wide, 0) == slot, 1.0, 0.0).astype(BF16)


def tokens_by_slots(ids_row, plane, experts, capacity):
    wide = (ids_row.shape[1], experts * capacity)
    slot = slot_of(column(ids_row), plane, experts, capacity, 0)
    return jnp.where(lax.broadcasted_iota(jnp.int32, wide, 1) == slot, 1.0, 0.0).astype(BF16)


def column(row):
    size = row.shape[1]
    diagonal = lax.broadcasted_iota(jnp.int32, (size, size), 0) == lax.broadcasted_iota(jnp.int32, (size, size), 1)
    return jnp.sum(jnp.where(diagonal, row, jnp.zeros_like(row)), axis=1, keepdims=True)


def unit_of(steer):
    return steer / jnp.sqrt(jnp.sum(steer * steer, axis=1, keepdims=True) + 1e-06)


def pieces(width):
    return [slice(at, at + COLS) for at in range(0, width, COLS)]


def gather_into(layout, tokens_at, blocks, capacity, width):
    for cols in pieces(width):
        rows = dot(layout, tokens_at(cols))
        for k, ref in blocks.items():
            ref[:, cols] = rows[k * capacity : (k + 1) * capacity].astype(BF16)


def sent_at(token_refs, weight_ref, steer_ref):
    unit = unit_of(steer_ref[...])

    def wide(cols):
        return jnp.concatenate([ref[:, cols].astype(F32) for ref in token_refs], axis=0)

    along = 0.0
    for cols in pieces(unit.shape[1]):
        along = along + jnp.sum(wide(cols) * unit[:, cols], axis=1, keepdims=True)
    weight = column(weight_ref[...])
    return lambda cols: (weight * (wide(cols) - along * unit[:, cols])).astype(BF16)


def pack_kernel(experts, capacity, at_ref, gate, up, saved_gate, saved_up, packed, kept):
    plane, chip, core = at_ref[0], at_ref[3], at_ref[4]
    size, width = gate.shape[1], gate.shape[0]
    count = CORES * experts * capacity
    packed[:width, :] = gate[...]
    packed[width : 2 * width, :] = up[...]
    wide = (capacity, saved_gate.shape[0])
    ahead = lax.broadcasted_iota(jnp.int32, wide, 1) - lax.broadcasted_iota(jnp.int32, wide, 0)

    def rows_of(core_index):
        chosen = []
        for chip_index in (chip, 1 - chip):
            for k in range(experts):
                source = jnp.where(plane < k, plane - k + experts, plane - k)
                start = ((source * 2 + chip_index) * CORES + core_index) * capacity
                chosen.append(jnp.where(ahead == start, 1.0, 0.0))
        return jnp.concatenate(chosen, axis=0).astype(BF16)

    chosen = rows_of(core)
    kept[:, :size] = dot(chosen, saved_gate[...]).astype(BF16)
    kept[:, size:] = dot(chosen, saved_up[...]).astype(BF16)
    chosen = rows_of(1 - core)
    start = packed.shape[0] - 2 * count
    packed[start : start + count, :] = dot(chosen, saved_gate[...]).astype(BF16)
    packed[start + count :, :] = dot(chosen, saved_up[...]).astype(BF16)


def saved_kernel(experts, capacity, at_ref, saved_gate, saved_up, kept, leaving):
    plane, chip, core = at_ref[0], at_ref[3], at_ref[4]
    size = saved_gate.shape[1]
    wide = (capacity, saved_gate.shape[0])
    ahead = lax.broadcasted_iota(jnp.int32, wide, 1) - lax.broadcasted_iota(jnp.int32, wide, 0)
    for ref, core_index in ((kept, core), (leaving, 1 - core)):
        chosen = []
        for chip_index in (chip, 1 - chip):
            for k in range(experts):
                source = jnp.where(plane < k, plane - k + experts, plane - k)
                start = ((source * 2 + chip_index) * CORES + core_index) * capacity
                chosen.append(jnp.where(ahead == start, 1.0, 0.0))
        chosen = jnp.concatenate(chosen, axis=0).astype(BF16)
        ref[:, :size] = dot(chosen, saved_gate[...]).astype(BF16)
        ref[:, size:] = dot(chosen, saved_up[...]).astype(BF16)


def first_kernel(ks, experts, capacity, at_ref, f_ids, b_ids, f_tok, b_tok, b_weight, steer, *out):
    blocks, width = dict(zip(ks, out)), f_tok.shape[1]

    @pl.when(at_ref[1] == 1)
    def _():
        layout = slots_by_tokens(b_ids[...], at_ref[0], experts, capacity)
        gather_into(layout, sent_at([b_tok], b_weight, steer), blocks, capacity, width)

    @pl.when(at_ref[1] == 0)
    def _():
        layout = slots_by_tokens(f_ids[...], at_ref[0], experts, capacity)
        gather_into(layout, lambda cols: f_tok[:, cols], blocks, capacity, width)


def rows_kernel(cuts, early, experts, capacity, at_ref, f_ids, b_ids, f_near, b_near, weight, steer, *refs):
    far, out = refs[: 2 * cuts], refs[2 * cuts :]
    width = f_near.shape[1]
    forward, backward = dict(enumerate(out[:experts])), dict(enumerate(out[experts:]))
    layout = slots_by_tokens(f_ids[...], at_ref[0], experts, capacity)

    @pl.when(at_ref[2] == 1)
    def _():
        gather_into(layout, lambda cols: f_near[:, cols], forward, capacity, width)

    @pl.when(at_ref[2] == 0)
    def _():
        gather_into(layout, lambda cols: jnp.concatenate([ref[:, cols] for ref in far[:cuts]], axis=0), forward, capacity, width)

    layout = slots_by_tokens(b_ids[...], at_ref[0], experts, capacity)

    @pl.when(at_ref[1] == 1)
    def _():
        others = {k: ref for k, ref in backward.items() if k not in early}
        gather_into(layout, sent_at([b_near], weight, steer), others, capacity, width)
        for k in early:
            backward[k][...] = forward[k][...]

    @pl.when(at_ref[1] == 0)
    def _():
        gather_into(layout, sent_at(far[cuts:], weight, steer), backward, capacity, width)


def forward_rows_kernel(experts, capacity, at_ref, ids, near, far, *out):
    blocks, width = dict(enumerate(out)), near.shape[1]
    layout = slots_by_tokens(ids[...], at_ref[0], experts, capacity)
    pl.when(at_ref[2] == 1)(lambda: gather_into(layout, lambda cols: near[:, cols], blocks, capacity, width))
    pl.when(at_ref[2] == 0)(lambda: gather_into(layout, lambda cols: far[:, cols], blocks, capacity, width))


def backward_rows_kernel(early, experts, capacity, at_ref, ids, near, weight, steer, far, *refs):
    swapped, out = refs[: len(early)], refs[len(early) :]
    blocks, width = dict(enumerate(out)), near.shape[1]
    layout = slots_by_tokens(ids[...], at_ref[0], experts, capacity)

    @pl.when(at_ref[1] == 1)
    def _():
        others = {k: ref for k, ref in blocks.items() if k not in early}
        gather_into(layout, sent_at([near], weight, steer), others, capacity, width)
        for k, ref in zip(early, swapped):
            blocks[k][...] = ref[...]

    @pl.when(at_ref[1] == 0)
    def _():
        gather_into(layout, sent_at([far], weight, steer), blocks, capacity, width)


def hidden_kernel(count, *refs):
    rows, weights = refs[: 2 * count], refs[2 * count : 2 * count + 4]
    own, other, x = refs[2 * count + 4 :]
    x[...] = stacked([ref[...] for ref in rows])
    half, size = own.shape[0], weights[0].shape[1]
    for j in range(CORES):
        value = jax.nn.silu(dot(x[...], weights[j][...])) * dot(x[...], weights[CORES + j][...])
        cols = slice(j * size, (j + 1) * size)
        own[:, cols], other[:, cols] = value[:half].astype(BF16), value[half:].astype(BF16)


def out_kernel(capacity, own, other, d0, d1, *refs):
    d2, d3, out = refs[:PARTS], refs[PARTS : 2 * PARTS], refs[2 * PARTS :]
    size = d0.shape[0]
    for cols in pieces(d0.shape[1]):
        rows = dot(own[:, :size], d0[:, cols]) + dot(own[:, size:], d1[:, cols])
        rows = rows + dot(other[:, :size], stacked([ref[:, cols] for ref in d2]))
        rows = rows + dot(other[:, size:], stacked([ref[:, cols] for ref in d3]))
        for i, ref in enumerate(out):
            ref[:, cols] = rows[i * capacity : (i + 1) * capacity].astype(BF16)


def grad_hidden_kernel(*refs):
    rows, downs, (own, other, x) = refs[: -5 - 2 * PARTS], refs[-5 - 2 * PARTS : -3], refs[-3:]
    x[...] = stacked([ref[...] for ref in rows])
    size = downs[0].shape[0]
    groups = (downs[2 : 2 + PARTS], downs[2 + PARTS :], downs[:1], downs[1:2])
    for j, group in enumerate(groups):
        grads = dot_rows(x[...], stacked([ref[...] for ref in group]))
        ref = other if j < 2 else own
        ref[:, (j % 2) * size : (j % 2 + 1) * size] = grads.astype(ref.dtype)


def grad_rows_kernel(capacity, got_count, side, grads, kept, *refs):
    got, (g0, g1, u0, u1) = refs[:got_count], refs[got_count : got_count + 4]
    out, (gate_grad, up_grad) = refs[got_count + 4 : -2], refs[-2:]
    size, height = g0.shape[1], grads.shape[0]
    here = slice(side * height, (side + 1) * height)
    theirs = (got[0][here, :size], got[0][here, size:]) if got_count == 1 else (got[0][...], got[1][...])
    saved = ((kept[here, :size], kept[here, size:]), theirs)
    for j, (g, u) in enumerate(saved):
        at = slice(j * size, (j + 1) * size)
        g, u = g.astype(F32), u.astype(F32)
        grad = grads[:, at].astype(F32)
        s = jax.nn.sigmoid(g)
        gate_grad[:, at] = (grad * u * s * (1.0 + g * (1.0 - s))).astype(BF16)
        up_grad[:, at] = (grad * g * s).astype(BF16)
    for cols in pieces(g0.shape[0]):
        rows = dot_rows(gate_grad[:, :size], g0[cols, :]) + dot_rows(gate_grad[:, size:], g1[cols, :])
        rows = rows + dot_rows(up_grad[:, :size], u0[cols, :]) + dot_rows(up_grad[:, size:], u1[cols, :])
        for i, ref in enumerate(out):
            ref[:, cols] = rows[i * capacity : (i + 1) * capacity].astype(ref.dtype)


def add_kernel(ours, theirs, out):
    out[...] = (ours[...] + theirs[...].astype(F32)).astype(BF16)


def forward_end_kernel(cuts, experts, capacity, at_ref, ids, near, weight, steer, *refs):
    far, back, (out, coefficient, mixed) = refs[:cuts], refs[cuts : cuts + experts], refs[cuts + experts :]
    layout = tokens_by_slots(ids[...], at_ref[0], experts, capacity)
    unit = unit_of(steer[...])
    along, scale = 0.0, column(weight[...])
    for cols in pieces(near.shape[1]):
        rows = scale * dot(layout, stacked([ref[:, cols] for ref in back]))
        mixed[:, cols] = rows
        along = along + jnp.sum(rows * unit[:, cols], axis=1, keepdims=True)
    size = along.shape[0]
    diagonal = lax.broadcasted_iota(jnp.int32, (size, size), 0) == lax.broadcasted_iota(jnp.int32, (size, size), 1)
    coefficient[...] = jnp.sum(jnp.where(diagonal, along, 0.0), axis=0, keepdims=True)

    def finish(*tokens):
        for cols in pieces(near.shape[1]):
            start = jnp.concatenate([ref[:, cols].astype(F32) for ref in tokens], axis=0)
            out[:, cols] = (start + mixed[:, cols] - along * unit[:, cols]).astype(BF16)

    pl.when(at_ref[2] == 1)(lambda: finish(near))
    pl.when(at_ref[2] == 0)(lambda: finish(*far))


def backward_end_kernel(cuts, experts, capacity, at_ref, ids, near, *refs):
    far, back, out = refs[:cuts], refs[cuts : cuts + experts], refs[cuts + experts]
    layout = tokens_by_slots(ids[...], at_ref[0], experts, capacity)

    def finish(*tokens):
        for cols in pieces(near.shape[1]):
            rows = dot(layout, stacked([ref[:, cols] for ref in back]))
            start = jnp.concatenate([ref[:, cols].astype(F32) for ref in tokens], axis=0)
            out[:, cols] = (start + rows).astype(BF16)

    pl.when(at_ref[1] == 1)(lambda: finish(near))
    pl.when(at_ref[1] == 0)(lambda: finish(*far))


def body(
    embedded,
    forward_held,
    forward_route,
    forward_weight,
    loss_cotangent,
    backward_held,
    backward_route,
    backward_weight,
    saved_gate,
    saved_up,
    gate_weight,
    up_weight,
    down_weight,
    steering,
):
    section_count = lax.axis_size("section")
    section_index = lax.axis_index("section")
    device_count = lax.axis_size("expert")
    device_index = lax.axis_index("expert")
    local_hidden = gate_weight.shape[2]
    holders = H // local_hidden
    experts = device_count // holders
    capacity = saved_gate.shape[1] // device_count
    rows = experts * capacity
    tokens, width = embedded.shape
    plane = device_index // holders
    chip = lax.rem(device_index, holders) // CORES
    core = lax.rem(device_index, CORES)
    first, last = section_index == 0, section_index == section_count - 1
    at = jnp.stack([plane, last.astype(jnp.int32), first.astype(jnp.int32), chip, core])
    early = [k for k in EARLY if k < experts]
    routed = [k for k in range(1, experts) if k not in early]

    def to_plane(value, by):
        pairs = [(i, (i + by * holders) % device_count) for i in range(device_count)]
        return lax.ppermute(value, "expert", pairs)

    def to_chip(value):
        pairs = [(i, i // holders * holders + (i + CORES) % holders) for i in range(device_count)]
        return lax.ppermute(value, "expert", pairs)

    def to_core(value):
        return lax.ppermute(value, "expert", [(i, i ^ 1) for i in range(device_count)])

    z_order, x_order = [], []

    def z_send(block, by, *deps):
        depth = OPT["z_depth"]
        out = to_plane(after(block, *z_order[-depth:][: len(z_order) >= depth], *deps), by)
        z_order.append(out)
        return out

    def x_send(block, *deps):
        depth = OPT["x_depth"]
        out = to_chip(after(block, *x_order[-depth:][: len(x_order) >= depth], *deps))
        x_order.append(out)
        return out

    def columns(height):
        return pl.BlockSpec((height, COLS), lambda i: (0, i))

    def whole(height, cols, index=0):
        return pl.BlockSpec((height, cols), lambda i: (index, 0))

    steps = width // COLS
    gate, up, down = gate_weight[0], up_weight[0], down_weight[0]
    f_ids, b_ids = forward_route[0].reshape(1, tokens), backward_route[0].reshape(1, tokens)
    f_weight, b_weight = forward_weight, backward_weight

    arriving = [shifted(forward_held, "section", 1)[0]]
    returning = [shifted(backward_held, "section", -1)[0]]
    d1 = to_core(down)
    part = local_hidden // PARTS
    d2 = []
    for p in range(PARTS):
        d2.append(to_chip(after(down, *d2[-1:])[p * part : (p + 1) * part]))
    if OPT["x_wd"]:
        x_order += d2
    core_first = () if OPT["pack"] else (to_core(gate), to_core(up))

    if section_count == 2:
        near_forward, near_backward = embedded, loss_cotangent
    else:
        near_forward = jnp.where(first, embedded, jnp.concatenate(arriving, axis=0))
        near_backward = jnp.where(last, loss_cotangent, jnp.concatenate(returning, axis=0))
    ones = call(
        functools.partial(first_kernel, early, experts, capacity),
        "first_rows",
        [shape(capacity, width)] * len(early),
        (at, f_ids, b_ids, near_forward, near_backward, b_weight, steering),
        in_specs=[SMEM] + [VMEM] * 6,
        limit=OPT["limit_first"],
    )
    got_one = {k: z_send(block, k, *(core_first if OPT["m_core"] else ())) for k, block in zip(early, ones)}

    def saved_rows(*deps):
        kept, leaving = call(
            functools.partial(saved_kernel, experts, capacity),
            "saved_rows",
            [shape(CORES * rows, 2 * local_hidden)] * 2,
            (at, after(saved_gate[0], *deps), saved_up[0]),
            in_specs=[SMEM] + [VMEM] * 2,
        )
        return kept, to_core(leaving)

    early_deps = list(got_one.values()) if OPT["rows_got"] else []
    if not OPT["pack"]:
        kept, got = saved_rows(*ones)
        if OPT["rows_core"]:
            early_deps += [got, *core_first]
    if OPT["rows_d1"]:
        early_deps.append(d1)
    if OPT["wd_first"]:
        early_deps.append(d2[0])
    ready = after(at, *early_deps)
    if OPT["split_rows"]:
        forward_rows = call(
            functools.partial(forward_rows_kernel, experts, capacity),
            "forward_rows",
            [shape(capacity, width)] * experts,
            (ready, f_ids, embedded, *arriving),
            in_specs=[SMEM] + [VMEM] * 3,
            limit=OPT["limit_rows"],
        )
        backward_rows = call(
            functools.partial(backward_rows_kernel, early, experts, capacity),
            "backward_rows",
            [shape(capacity, width)] * experts,
            (at, b_ids, loss_cotangent, b_weight, steering, *returning, *(forward_rows[k] for k in early)),
            in_specs=[SMEM] + [VMEM] * (5 + len(early)),
            limit=OPT["limit_rows"],
        )
    else:
        both = call(
            functools.partial(rows_kernel, 1, early, experts, capacity),
            "rows",
            [shape(capacity, width)] * (2 * experts),
            (ready, f_ids, b_ids, embedded, loss_cotangent, b_weight, steering, *arriving, *returning),
            in_specs=[SMEM] + [VMEM] * 8,
            limit=OPT["limit_rows"],
        )
        forward_rows, backward_rows = both[:experts], both[experts:]
    forward_got, backward_got = {0: forward_rows[0]}, {0: backward_rows[0]}
    for k in routed:
        forward_got[k] = z_send(forward_rows[k], k, *(backward_rows[:1] if OPT["br_dep"] else ()))
    across = {0: x_send(forward_got[0])}
    got_two = {k: z_send(backward_rows[k], k) for k in early}

    if OPT["pack"]:
        saved_block = pl.cdiv(2 * width, rows)
        packed, kept = call(
            functools.partial(pack_kernel, experts, capacity),
            "packed",
            [shape((saved_block + 2 * CORES) * rows, local_hidden), shape(CORES * rows, 2 * local_hidden)],
            (at, gate, up, saved_gate[0], after(saved_up[0], *forward_rows)),
            in_specs=[SMEM] + [VMEM] * 4,
            limit=40,
        )
        sibling = to_core(packed)
    anchors = [(), tuple(got_two.values()), tuple(forward_got[k] for k in routed), (across[0],)]
    d3 = [to_core(after(each, *anchors[OPT["d3_after"]])) for each in d2]

    for k in routed:
        across[k] = x_send(forward_got[k])
        backward_got[k] = z_send(backward_rows[k], k)
    for k in early:
        forward_got[k] = jnp.where(last, got_two[k], got_one[k])
        backward_got[k] = jnp.where(last, got_one[k], got_two[k])
        across[k] = x_send(forward_got[k])

    columns_of = (gate, core_first[0], up, core_first[1])
    saved_args = (kept, got)
    downs = (down, d1, *d2, *d3)

    def hidden_of(group, *deps):
        count = len(group)
        height = count * capacity
        return call(
            functools.partial(hidden_kernel, count),
            "hidden",
            [shape(height, 2 * local_hidden)] * 2,
            [after(forward_got[group[0]], *deps)]
            + [forward_got[k] for k in group[1:]]
            + [across[k] for k in group]
            + list(columns_of),
            limit=OPT["limit_mm"],
            in_specs=[VMEM] * (2 * count + 4),
            scratch=[pltpu.VMEM((2 * height, width), BF16)],
        )

    def out_of(group, own, other):
        height = len(group) * capacity
        return call(
            functools.partial(out_kernel, capacity),
            "expert_out",
            [shape(capacity, width)] * len(group),
            (own, other, *downs),
            limit=OPT["limit_mm"],
            in_specs=[VMEM] * (2 + len(downs)),
        )

    groups = [g for g in ([0] + routed, early) if g]
    if OPT["one_group"]:
        groups = [list(range(experts))]
    forward_back = {}
    marks = [()]
    for group in groups:
        own, other = hidden_of(group, *marks[min(OPT["h2_after"], len(marks) - 1)])
        marks.append((other,))
        blocks = out_of(group, own, x_send(other))
        marks.append((blocks[0],))
        for k, block in zip(group, blocks):
            forward_back[k] = block if k == 0 else z_send(block, -k)

    gh_after = marks[min(OPT["gh_after"], len(marks) - 1)]
    grads_own, grads_other = call(
        grad_hidden_kernel,
        "grad_hidden",
        [shape(rows, 2 * local_hidden, F32), shape(rows, 2 * local_hidden)],
        [after(backward_got[0], *gh_after)] + [backward_got[k] for k in range(1, experts)] + list(downs),
        limit=OPT["limit_mm"],
        in_specs=[VMEM] * (experts + len(downs)),
        scratch=[pltpu.VMEM((rows, width), BF16)],
    )
    grads_got = x_send(grads_other)

    def grad_rows(grads, side, outs):
        return call(
            functools.partial(grad_rows_kernel, capacity, len(saved_args) - 1, side),
            "grad_rows",
            outs,
            (grads, *saved_args, *columns_of),
            limit=OPT["limit_mm"],
            in_specs=[VMEM] * (6 + len(saved_args) - 1 + 0),
            scratch=[pltpu.VMEM((rows, 2 * local_hidden), BF16)] * 2,
        )

    mine = grad_rows(grads_own, 0, [shape(capacity, width, F32)] * experts)
    if OPT["mine_first"]:
        grads_got = after(grads_got, *mine)
    grads_got = after(grads_got, *marks[min(OPT["theirs_after"], len(marks) - 1)])
    theirs = grad_rows(grads_got, 1, [shape(capacity, width)] * experts)
    backward_back = {}
    ahead = [k for k in OPT["rs_order"] if k < experts]
    for k in ahead + [k for k in range(experts) if k not in ahead]:
        block = call(add_kernel, "add_rows", [shape(capacity, width)], (mine[k], x_send(theirs[k])), in_specs=[VMEM] * 2, limit=OPT["limit_add"])[0]
        backward_back[k] = block if k == 0 else z_send(block, -k)

    forward_out, coefficient = call(
        functools.partial(forward_end_kernel, len(arriving), experts, capacity),
        "forward_end",
        [shape(tokens, width), shape(1, tokens, F32)],
        (at, f_ids, embedded, f_weight, steering, *arriving, *(forward_back[k] for k in range(experts))),
        in_specs=[SMEM] + [VMEM] * (4 + len(arriving) + experts),
        scratch=[pltpu.VMEM((tokens, width), F32)],
    )
    backward_out = call(
        functools.partial(backward_end_kernel, len(arriving), experts, capacity),
        "backward_end",
        [shape(tokens, width)],
        (at, b_ids, loss_cotangent, *returning, *(backward_back[k] for k in range(experts))),
        in_specs=[SMEM] + [VMEM] * (2 + len(arriving) + experts),
    )[0]
    return (forward_out[None], coefficient, backward_out[None])


def solution(mesh):
    in_specs = (
        P("expert", None),
        P("section", "expert", None),
        P("section", "expert", None),
        P("section", "expert"),
        P("expert", None),
        P("section", "expert", None),
        P("section", "expert", None),
        P("section", "expert"),
        P("section", None, "expert"),
        P("section", None, "expert"),
        P("section", None, "expert"),
        P("section", None, "expert"),
        P("section", "expert", None),
        P("section", None),
    )
    out_specs = (P("section", "expert", None), P("section", "expert"), P("section", "expert", None))
    return jax.shard_map(body, mesh=mesh, in_specs=in_specs, out_specs=out_specs, check_vma=False)
```

```python
import functools

import jax
import jax.numpy as jnp
from jax import lax
from jax.experimental import pallas as pl
from jax.experimental.pallas import tpu as pltpu
from jax.sharding import PartitionSpec as P

H = 1024
CORES = 2
EARLY = (2,)
DOWN_PARTS = 2
RETURN_ORDER = (2, 1, 3, 0)
FLOPS = {"grad_rows": 10000000000, "add_rows": 2000000000, "forward_end": 50000000000}
BF16 = jnp.bfloat16
F32 = jnp.float32
COLS = 896
ROWS_BY_ROWS = (((1,), (1,)), ((), ()))
SMEM = pl.BlockSpec(memory_space=pltpu.SMEM)
VMEM = pl.BlockSpec(memory_space=pltpu.VMEM)


def after(value, *deps):
    return lax.optimization_barrier((value, *deps))[0] if deps else value


def dot(a, b):
    return jnp.dot(a, b, preferred_element_type=F32)


def dot_rows(a, b):
    return lax.dot_general(a, b, ROWS_BY_ROWS, preferred_element_type=F32)


def shape(rows, cols, dtype=BF16):
    return jax.ShapeDtypeStruct((rows, cols), dtype)


def shifted(value, axis, by):
    devices = lax.axis_size(axis)
    pairs = [(i, i + by) for i in range(devices) if 0 <= i + by < devices]
    return lax.ppermute(value, axis, pairs)


def call(kernel, name, outs, args, grid=None, in_specs=None, out_specs=None, scratch=(), limit=24):
    extra = {} if grid is None else {"grid": grid}
    return pl.pallas_call(
        kernel,
        out_shape=outs,
        in_specs=in_specs,
        out_specs=out_specs if out_specs is not None else [VMEM] * len(outs),
        scratch_shapes=list(scratch),
        name=name,
        cost_estimate=pl.CostEstimate(flops=FLOPS.get(name, 5000000000), bytes_accessed=100000, transcendentals=0),
        compiler_params=pltpu.CompilerParams(vmem_limit_bytes=limit << 20),
        **extra,
    )(*args)


def stacked(values):
    if values[0].shape[0] % 16 == 0:
        return jnp.concatenate(values, axis=0)
    return jnp.concatenate([value.astype(F32) for value in values], axis=0).astype(BF16)


def slot_of(ids, plane, experts, capacity, axis):
    tokens = ids.shape[axis]
    wide = (tokens, 128) if axis == 0 else (max(8, experts), tokens)
    chosen = jnp.where(ids == lax.broadcasted_iota(jnp.int32, wide, 1 - axis), 1.0, 0.0)
    row = lax.broadcasted_iota(jnp.int32, (tokens, tokens), 0)
    col = lax.broadcasted_iota(jnp.int32, (tokens, tokens), 1)
    if axis == 0:
        earlier = dot(jnp.where(col < row, 1.0, 0.0).astype(BF16), chosen.astype(BF16))
    else:
        earlier = dot(chosen.astype(BF16), jnp.where(row < col, 1.0, 0.0).astype(BF16))
    position = jnp.sum(chosen * earlier, axis=1 - axis, keepdims=True).astype(jnp.int32)
    ahead = ids - plane
    return jnp.where(ahead < 0, ahead + experts, ahead) * capacity + position


def slots_by_tokens(ids_row, plane, experts, capacity):
    wide = (experts * capacity, ids_row.shape[1])
    slot = slot_of(ids_row, plane, experts, capacity, 1)
    return jnp.where(lax.broadcasted_iota(jnp.int32, wide, 0) == slot, 1.0, 0.0).astype(BF16)


def tokens_by_slots(ids_row, plane, experts, capacity):
    wide = (ids_row.shape[1], experts * capacity)
    slot = slot_of(column(ids_row), plane, experts, capacity, 0)
    return jnp.where(lax.broadcasted_iota(jnp.int32, wide, 1) == slot, 1.0, 0.0).astype(BF16)


def column(row):
    size = row.shape[1]
    diagonal = lax.broadcasted_iota(jnp.int32, (size, size), 0) == lax.broadcasted_iota(jnp.int32, (size, size), 1)
    return jnp.sum(jnp.where(diagonal, row, jnp.zeros_like(row)), axis=1, keepdims=True)


def unit_of(steer):
    return steer / jnp.sqrt(jnp.sum(steer * steer, axis=1, keepdims=True) + 1e-06)


def pieces(width):
    return [slice(at, at + COLS) for at in range(0, width, COLS)]


def gather_into(layout, tokens_at, blocks, capacity, width):
    for cols in pieces(width):
        rows = dot(layout, tokens_at(cols))
        for k, ref in blocks.items():
            ref[:, cols] = rows[k * capacity : (k + 1) * capacity].astype(BF16)


def sent_at(token_ref, weight_ref, steer_ref):
    unit = unit_of(steer_ref[...])

    def wide(cols):
        return token_ref[:, cols].astype(F32)

    along = 0.0
    for cols in pieces(unit.shape[1]):
        along = along + jnp.sum(wide(cols) * unit[:, cols], axis=1, keepdims=True)
    weight = column(weight_ref[...])
    return lambda cols: (weight * (wide(cols) - along * unit[:, cols])).astype(BF16)


def saved_kernel(experts, capacity, at_ref, saved_gate, saved_up, kept, leaving):
    plane, chip, core = at_ref[0], at_ref[3], at_ref[4]
    size = saved_gate.shape[1]
    wide = (capacity, saved_gate.shape[0])
    ahead = lax.broadcasted_iota(jnp.int32, wide, 1) - lax.broadcasted_iota(jnp.int32, wide, 0)
    for ref, core_index in ((kept, core), (leaving, 1 - core)):
        chosen = []
        for chip_index in (chip, 1 - chip):
            for k in range(experts):
                source = jnp.where(plane < k, plane - k + experts, plane - k)
                start = ((source * 2 + chip_index) * CORES + core_index) * capacity
                chosen.append(jnp.where(ahead == start, 1.0, 0.0))
        chosen = jnp.concatenate(chosen, axis=0).astype(BF16)
        ref[:, :size] = dot(chosen, saved_gate[...]).astype(BF16)
        ref[:, size:] = dot(chosen, saved_up[...]).astype(BF16)


def first_kernel(ks, experts, capacity, at_ref, f_ids, b_ids, f_tok, b_tok, b_weight, steer, *out):
    blocks, width = dict(zip(ks, out)), f_tok.shape[1]

    @pl.when(at_ref[1] == 1)
    def _():
        layout = slots_by_tokens(b_ids[...], at_ref[0], experts, capacity)
        gather_into(layout, sent_at(b_tok, b_weight, steer), blocks, capacity, width)

    @pl.when(at_ref[1] == 0)
    def _():
        layout = slots_by_tokens(f_ids[...], at_ref[0], experts, capacity)
        gather_into(layout, lambda cols: f_tok[:, cols], blocks, capacity, width)


def forward_rows_kernel(experts, capacity, at_ref, ids, near, far, *out):
    blocks, width = dict(enumerate(out)), near.shape[1]
    layout = slots_by_tokens(ids[...], at_ref[0], experts, capacity)
    pl.when(at_ref[2] == 1)(lambda: gather_into(layout, lambda cols: near[:, cols], blocks, capacity, width))
    pl.when(at_ref[2] == 0)(lambda: gather_into(layout, lambda cols: far[:, cols], blocks, capacity, width))


def backward_rows_kernel(early, experts, capacity, at_ref, ids, near, weight, steer, far, *refs):
    swapped, out = refs[: len(early)], refs[len(early) :]
    blocks, width = dict(enumerate(out)), near.shape[1]
    layout = slots_by_tokens(ids[...], at_ref[0], experts, capacity)

    @pl.when(at_ref[1] == 1)
    def _():
        others = {k: ref for k, ref in blocks.items() if k not in early}
        gather_into(layout, sent_at(near, weight, steer), others, capacity, width)
        for k, ref in zip(early, swapped):
            blocks[k][...] = ref[...]

    @pl.when(at_ref[1] == 0)
    def _():
        gather_into(layout, sent_at(far, weight, steer), blocks, capacity, width)


def hidden_kernel(count, *refs):
    rows, weights = refs[:count], refs[count : count + 4]
    own, other, x = refs[count + 4 :]
    x[...] = stacked([ref[...] for ref in rows])
    half, size = own.shape[0], weights[0].shape[1]
    for j in range(CORES):
        value = jax.nn.silu(dot(x[...], weights[j][...])) * dot(x[...], weights[CORES + j][...])
        cols = slice(j * size, (j + 1) * size)
        own[:, cols], other[:, cols] = value[:half].astype(BF16), value[half:].astype(BF16)


def out_kernel(capacity, own, other, d0, d1, *refs):
    d2, d3, out = refs[0], refs[1 : 1 + DOWN_PARTS], refs[1 + DOWN_PARTS :]
    size = d0.shape[0]
    for cols in pieces(d0.shape[1]):
        rows = dot(own[:, :size], d0[:, cols]) + dot(own[:, size:], d1[:, cols])
        rows = rows + dot(other[:, :size], d2[:, cols])
        rows = rows + dot(other[:, size:], stacked([ref[:, cols] for ref in d3]))
        for i, ref in enumerate(out):
            ref[:, cols] = rows[i * capacity : (i + 1) * capacity].astype(BF16)


def grad_hidden_kernel(*refs):
    rows, downs, (own, other, x) = refs[: -6 - DOWN_PARTS], refs[-6 - DOWN_PARTS : -3], refs[-3:]
    x[...] = stacked([ref[...] for ref in rows])
    size = downs[0].shape[0]
    groups = (downs[2:3], downs[3:], downs[:1], downs[1:2])
    for j, group in enumerate(groups):
        grads = dot_rows(x[...], stacked([ref[...] for ref in group]))
        ref = other if j < 2 else own
        ref[:, (j % 2) * size : (j % 2 + 1) * size] = grads.astype(ref.dtype)


def grad_rows_kernel(capacity, order, side, grads, kept, got, g0, g1, u0, u1, *refs):
    out, (gate_grad, up_grad) = refs[:-2], refs[-2:]
    size, height = g0.shape[1], grads.shape[0]
    here = slice(side * height, (side + 1) * height)
    for j, saved in enumerate((kept, got)):
        at = slice(j * size, (j + 1) * size)
        g, u = saved[here, :size].astype(F32), saved[here, size:].astype(F32)
        grad = grads[:, at].astype(F32)
        s = jax.nn.sigmoid(g)
        gate_grad[:, at] = (grad * u * s * (1.0 + g * (1.0 - s))).astype(BF16)
        up_grad[:, at] = (grad * g * s).astype(BF16)
    for cols in pieces(g0.shape[0]):
        rows = dot_rows(gate_grad[:, :size], g0[cols, :]) + dot_rows(gate_grad[:, size:], g1[cols, :])
        rows = rows + dot_rows(up_grad[:, :size], u0[cols, :]) + dot_rows(up_grad[:, size:], u1[cols, :])
        for ref, k in zip(out, order):
            ref[:, cols] = rows[k * capacity : (k + 1) * capacity].astype(ref.dtype)


def add_kernel(ours, theirs, out):
    out[...] = (ours[...] + theirs[...].astype(F32)).astype(BF16)


def forward_end_kernel(experts, capacity, at_ref, ids, near, far, weight, steer, *refs):
    back, (out, coefficient, mixed) = refs[:experts], refs[experts:]
    layout = tokens_by_slots(ids[...], at_ref[0], experts, capacity)
    unit = unit_of(steer[...])
    along, scale = 0.0, column(weight[...])
    for cols in pieces(near.shape[1]):
        rows = scale * dot(layout, stacked([ref[:, cols] for ref in back]))
        mixed[:, cols] = rows
        along = along + jnp.sum(rows * unit[:, cols], axis=1, keepdims=True)
    size = along.shape[0]
    diagonal = lax.broadcasted_iota(jnp.int32, (size, size), 0) == lax.broadcasted_iota(jnp.int32, (size, size), 1)
    coefficient[...] = jnp.sum(jnp.where(diagonal, along, 0.0), axis=0, keepdims=True)

    def finish(tokens):
        for cols in pieces(near.shape[1]):
            start = tokens[:, cols].astype(F32)
            out[:, cols] = (start + mixed[:, cols] - along * unit[:, cols]).astype(BF16)

    pl.when(at_ref[2] == 1)(lambda: finish(near))
    pl.when(at_ref[2] == 0)(lambda: finish(far))


def backward_end_kernel(experts, capacity, at_ref, ids, near, far, *refs):
    back, out = refs[:experts], refs[experts]
    layout = tokens_by_slots(ids[...], at_ref[0], experts, capacity)

    def finish(tokens):
        for cols in pieces(near.shape[1]):
            rows = dot(layout, stacked([ref[:, cols] for ref in back]))
            start = tokens[:, cols].astype(F32)
            out[:, cols] = (start + rows).astype(BF16)

    pl.when(at_ref[1] == 1)(lambda: finish(near))
    pl.when(at_ref[1] == 0)(lambda: finish(far))


def body(
    embedded,
    forward_held,
    forward_route,
    forward_weight,
    loss_cotangent,
    backward_held,
    backward_route,
    backward_weight,
    saved_gate,
    saved_up,
    gate_weight,
    up_weight,
    down_weight,
    steering,
):
    section_count = lax.axis_size("section")
    section_index = lax.axis_index("section")
    device_count = lax.axis_size("expert")
    device_index = lax.axis_index("expert")
    local_hidden = gate_weight.shape[2]
    holders = H // local_hidden
    experts = device_count // holders
    capacity = saved_gate.shape[1] // device_count
    rows = experts * capacity
    tokens, width = embedded.shape
    plane = device_index // holders
    chip = lax.rem(device_index, holders) // CORES
    core = lax.rem(device_index, CORES)
    first, last = section_index == 0, section_index == section_count - 1
    at = jnp.stack([plane, last.astype(jnp.int32), first.astype(jnp.int32), chip, core])
    early = [k for k in EARLY if k < experts]
    routed = [k for k in range(1, experts) if k not in early]

    def to_plane(value, by):
        pairs = [(i, (i + by * holders) % device_count) for i in range(device_count)]
        return lax.ppermute(value, "expert", pairs)

    def to_chip(value):
        pairs = [(i, i // holders * holders + (i + CORES) % holders) for i in range(device_count)]
        return lax.ppermute(value, "expert", pairs)

    def to_core(value):
        return lax.ppermute(value, "expert", [(i, i ^ 1) for i in range(device_count)])

    z_order, x_order = [], []

    def z_send(block, by, *deps, ahead=3):
        out = to_plane(after(block, *z_order[-ahead:][: len(z_order) >= ahead], *deps), by)
        z_order.append(out)
        return out

    def x_send(block):
        out = to_chip(after(block, *x_order[-2:][: len(x_order) >= 2]))
        x_order.append(out)
        return out

    gate, up, down = gate_weight[0], up_weight[0], down_weight[0]
    f_ids, b_ids = forward_route[0].reshape(1, tokens), backward_route[0].reshape(1, tokens)

    arriving = shifted(forward_held, "section", 1)[0]
    returning = shifted(backward_held, "section", -1)[0]
    d2 = to_chip(down)
    gate_sib, up_sib = to_core(gate), to_core(up)

    if section_count == 2:
        near_forward, near_backward = embedded, loss_cotangent
    else:
        near_forward = jnp.where(first, embedded, arriving)
        near_backward = jnp.where(last, loss_cotangent, returning)
    ones = call(
        functools.partial(first_kernel, early, experts, capacity),
        "first_rows",
        [shape(capacity, width)] * len(early),
        (at, f_ids, b_ids, near_forward, near_backward, backward_weight, steering),
        in_specs=[SMEM] + [VMEM] * 6,
        limit=56,
    )
    got_one = {k: z_send(block, k, gate_sib, up_sib) for k, block in zip(early, ones)}
    d1 = to_core(down)
    forward_rows = call(
        functools.partial(forward_rows_kernel, experts, capacity),
        "forward_rows",
        [shape(capacity, width)] * experts,
        (after(at, gate_sib, up_sib, d1), f_ids, embedded, arriving),
        in_specs=[SMEM] + [VMEM] * 3,
    )
    backward_rows = call(
        functools.partial(backward_rows_kernel, early, experts, capacity),
        "backward_rows",
        [shape(capacity, width)] * experts,
        (at, b_ids, loss_cotangent, backward_weight, steering, returning, *(forward_rows[k] for k in early)),
        in_specs=[SMEM] + [VMEM] * (5 + len(early)),
    )
    forward_got, backward_got = {0: forward_rows[0]}, {0: backward_rows[0]}
    for k in routed:
        forward_got[k] = z_send(forward_rows[k], k)
    got_two = {k: z_send(backward_rows[k], k) for k in early}

    kept, leaving = call(
        functools.partial(saved_kernel, experts, capacity),
        "saved_rows",
        [shape(CORES * rows, 2 * local_hidden)] * 2,
        (at, after(saved_gate[0], backward_rows[0]), saved_up[0]),
        in_specs=[SMEM] + [VMEM] * 2,
    )
    got = to_core(leaving)
    held = after(d2, *(forward_got[k] for k in routed))
    height = local_hidden // DOWN_PARTS
    d3 = [to_core(held[p * height : (p + 1) * height]) for p in range(DOWN_PARTS)]

    across = {}
    for k in routed:
        across[k] = x_send(forward_got[k])
        backward_got[k] = z_send(backward_rows[k], k, ahead=1)
    for k in early:
        forward_got[k] = jnp.where(last, got_two[k], got_one[k])
        backward_got[k] = jnp.where(last, got_one[k], got_two[k])
        across[k] = x_send(forward_got[k])
    across[0] = x_send(forward_got[0])
    columns_of = (gate, gate_sib, up, up_sib)
    downs = (down, d1, d2, *d3)

    forward_back, outs = {}, []
    for group in [each for each in (routed, early + [0]) if each]:
        height = len(group) * capacity
        own, other = call(
            functools.partial(hidden_kernel, 2 * len(group)),
            "hidden",
            [shape(height, 2 * local_hidden)] * 2,
            [after(forward_got[group[0]], got)]
            + [forward_got[k] for k in group[1:]]
            + [across[k] for k in group]
            + list(columns_of),
            in_specs=[VMEM] * (2 * len(group) + 4),
            scratch=[pltpu.VMEM((2 * height, width), BF16)],
            limit=16,
        )
        blocks = call(
            functools.partial(out_kernel, capacity),
            "expert_out",
            [shape(capacity, width)] * len(group),
            (own, x_send(other), *downs),
            in_specs=[VMEM] * (2 + len(downs)),
            limit=16,
        )
        outs.append(blocks[0])
        for k, block in zip(group, blocks):
            forward_back[k] = block if k == 0 else z_send(block, -k)

    grads_own, grads_other = call(
        grad_hidden_kernel,
        "grad_hidden",
        [shape(rows, 2 * local_hidden, F32), shape(rows, 2 * local_hidden)],
        [after(backward_got[0], outs[0])] + [backward_got[k] for k in range(1, experts)] + list(downs),
        in_specs=[VMEM] * (experts + len(downs)),
        scratch=[pltpu.VMEM((rows, width), BF16)],
        limit=16,
    )
    grads_got = x_send(grads_other)

    def grad_rows(grads, side, order, dtype):
        return call(
            functools.partial(grad_rows_kernel, capacity, order, side),
            "grad_rows",
            [shape(capacity, width, dtype)] * experts,
            (grads, kept, got, *columns_of),
            in_specs=[VMEM] * 7,
            scratch=[pltpu.VMEM((rows, 2 * local_hidden), BF16)] * 2,
            limit=16,
        )

    mine = grad_rows(grads_own, 0, list(range(experts)), F32)
    order = [k for k in RETURN_ORDER if k < experts]
    order += [k for k in range(experts) if k not in order]
    theirs = grad_rows(grads_got, 1, order, BF16)
    backward_back = {}
    for k, part in zip(order, theirs):
        block = call(add_kernel, "add_rows", [shape(capacity, width)], (mine[k], x_send(part)), in_specs=[VMEM] * 2)[0]
        backward_back[k] = block if k == 0 else z_send(block, -k)

    forward_out, coefficient = call(
        functools.partial(forward_end_kernel, experts, capacity),
        "forward_end",
        [shape(tokens, width), shape(1, tokens, F32)],
        (at, f_ids, embedded, arriving, forward_weight, steering, *(forward_back[k] for k in range(experts))),
        in_specs=[SMEM] + [VMEM] * (5 + experts),
        scratch=[pltpu.VMEM((tokens, width), F32)],
    )
    backward_out = call(
        functools.partial(backward_end_kernel, experts, capacity),
        "backward_end",
        [shape(tokens, width)],
        (at, b_ids, loss_cotangent, returning, *(backward_back[k] for k in range(experts))),
        in_specs=[SMEM] + [VMEM] * (3 + experts),
    )[0]
    return (forward_out[None], coefficient, backward_out[None])


def solution(mesh):
    in_specs = (
        P("expert", None),
        P("section", "expert", None),
        P("section", "expert", None),
        P("section", "expert"),
        P("expert", None),
        P("section", "expert", None),
        P("section", "expert", None),
        P("section", "expert"),
        P("section", None, "expert"),
        P("section", None, "expert"),
        P("section", None, "expert"),
        P("section", None, "expert"),
        P("section", "expert", None),
        P("section", None),
    )
    out_specs = (P("section", "expert", None), P("section", "expert"), P("section", "expert", None))
    return jax.shard_map(body, mesh=mesh, in_specs=in_specs, out_specs=out_specs, check_vma=False)
```

```python
import functools

import jax
import jax.numpy as jnp
from jax import lax
from jax.experimental import pallas as pl
from jax.experimental.pallas import tpu as pltpu
from jax.sharding import PartitionSpec as P

H = 1024
CORES = 2
EARLY = (2,)
DOWN_PARTS = 2
RETURN_ORDER = (2, 1, 3, 0)
FLOPS = {"grad_rows": 10000000000, "add_rows": 2000000000, "forward_end": 50000000000}
BF16 = jnp.bfloat16
F32 = jnp.float32
COLS = 896
ROWS_BY_ROWS = (((1,), (1,)), ((), ()))
SMEM = pl.BlockSpec(memory_space=pltpu.SMEM)
VMEM = pl.BlockSpec(memory_space=pltpu.VMEM)


def after(value, *deps):
    return lax.optimization_barrier((value, *deps))[0] if deps else value


def dot(a, b):
    return jnp.dot(a, b, preferred_element_type=F32)


def dot_rows(a, b):
    return lax.dot_general(a, b, ROWS_BY_ROWS, preferred_element_type=F32)


def shape(rows, cols, dtype=BF16):
    return jax.ShapeDtypeStruct((rows, cols), dtype)


def shifted(value, axis, by):
    devices = lax.axis_size(axis)
    pairs = [(i, i + by) for i in range(devices) if 0 <= i + by < devices]
    return lax.ppermute(value, axis, pairs)


def call(kernel, name, outs, args, grid=None, in_specs=None, out_specs=None, scratch=(), limit=24):
    extra = {} if grid is None else {"grid": grid}
    return pl.pallas_call(
        kernel,
        out_shape=outs,
        in_specs=in_specs,
        out_specs=out_specs if out_specs is not None else [VMEM] * len(outs),
        scratch_shapes=list(scratch),
        name=name,
        cost_estimate=pl.CostEstimate(flops=FLOPS.get(name, 5000000000), bytes_accessed=100000, transcendentals=0),
        compiler_params=pltpu.CompilerParams(vmem_limit_bytes=limit << 20),
        **extra,
    )(*args)


def stacked(values):
    if values[0].shape[0] % 16 == 0:
        return jnp.concatenate(values, axis=0)
    return jnp.concatenate([value.astype(F32) for value in values], axis=0).astype(BF16)


def slot_of(ids, plane, experts, capacity, axis):
    tokens = ids.shape[axis]
    wide = (tokens, 128) if axis == 0 else (max(8, experts), tokens)
    chosen = jnp.where(ids == lax.broadcasted_iota(jnp.int32, wide, 1 - axis), 1.0, 0.0)
    row = lax.broadcasted_iota(jnp.int32, (tokens, tokens), 0)
    col = lax.broadcasted_iota(jnp.int32, (tokens, tokens), 1)
    if axis == 0:
        earlier = dot(jnp.where(col < row, 1.0, 0.0).astype(BF16), chosen.astype(BF16))
    else:
        earlier = dot(chosen.astype(BF16), jnp.where(row < col, 1.0, 0.0).astype(BF16))
    position = jnp.sum(chosen * earlier, axis=1 - axis, keepdims=True).astype(jnp.int32)
    ahead = ids - plane
    return jnp.where(ahead < 0, ahead + experts, ahead) * capacity + position


def slots_by_tokens(ids_row, plane, experts, capacity):
    wide = (experts * capacity, ids_row.shape[1])
    slot = slot_of(ids_row, plane, experts, capacity, 1)
    return jnp.where(lax.broadcasted_iota(jnp.int32, wide, 0) == slot, 1.0, 0.0).astype(BF16)


def tokens_by_slots(ids_row, plane, experts, capacity):
    wide = (ids_row.shape[1], experts * capacity)
    slot = slot_of(column(ids_row), plane, experts, capacity, 0)
    return jnp.where(lax.broadcasted_iota(jnp.int32, wide, 1) == slot, 1.0, 0.0).astype(BF16)


def column(row):
    size = row.shape[1]
    diagonal = lax.broadcasted_iota(jnp.int32, (size, size), 0) == lax.broadcasted_iota(jnp.int32, (size, size), 1)
    return jnp.sum(jnp.where(diagonal, row, jnp.zeros_like(row)), axis=1, keepdims=True)


def unit_of(steer):
    return steer / jnp.sqrt(jnp.sum(steer * steer, axis=1, keepdims=True) + 1e-06)


def pieces(width):
    return [slice(at, at + COLS) for at in range(0, width, COLS)]


def gather_into(layout, tokens_at, blocks, capacity, width):
    for cols in pieces(width):
        rows = dot(layout, tokens_at(cols))
        for k, ref in blocks.items():
            ref[:, cols] = rows[k * capacity : (k + 1) * capacity].astype(BF16)


def sent_at(token_ref, weight_ref, steer_ref):
    unit = unit_of(steer_ref[...])

    def wide(cols):
        return token_ref[:, cols].astype(F32)

    along = 0.0
    for cols in pieces(unit.shape[1]):
        along = along + jnp.sum(wide(cols) * unit[:, cols], axis=1, keepdims=True)
    weight = column(weight_ref[...])
    return lambda cols: (weight * (wide(cols) - along * unit[:, cols])).astype(BF16)


def saved_kernel(experts, capacity, at_ref, saved_gate, saved_up, kept, leaving):
    plane, chip, core = at_ref[0], at_ref[3], at_ref[4]
    size = saved_gate.shape[1]
    wide = (capacity, saved_gate.shape[0])
    ahead = lax.broadcasted_iota(jnp.int32, wide, 1) - lax.broadcasted_iota(jnp.int32, wide, 0)
    for ref, core_index in ((kept, core), (leaving, 1 - core)):
        chosen = []
        for chip_index in (chip, 1 - chip):
            for k in range(experts):
                source = jnp.where(plane < k, plane - k + experts, plane - k)
                start = ((source * 2 + chip_index) * CORES + core_index) * capacity
                chosen.append(jnp.where(ahead == start, 1.0, 0.0))
        chosen = jnp.concatenate(chosen, axis=0).astype(BF16)
        ref[:, :size] = dot(chosen, saved_gate[...]).astype(BF16)
        ref[:, size:] = dot(chosen, saved_up[...]).astype(BF16)


def first_kernel(ks, experts, capacity, at_ref, f_ids, b_ids, f_tok, b_tok, b_weight, steer, *out):
    blocks, width = dict(zip(ks, out)), f_tok.shape[1]

    @pl.when(at_ref[1] == 1)
    def _():
        layout = slots_by_tokens(b_ids[...], at_ref[0], experts, capacity)
        gather_into(layout, sent_at(b_tok, b_weight, steer), blocks, capacity, width)

    @pl.when(at_ref[1] == 0)
    def _():
        layout = slots_by_tokens(f_ids[...], at_ref[0], experts, capacity)
        gather_into(layout, lambda cols: f_tok[:, cols], blocks, capacity, width)


def forward_rows_kernel(experts, capacity, at_ref, ids, near, far, *out):
    blocks, width = dict(enumerate(out)), near.shape[1]
    layout = slots_by_tokens(ids[...], at_ref[0], experts, capacity)
    pl.when(at_ref[2] == 1)(lambda: gather_into(layout, lambda cols: near[:, cols], blocks, capacity, width))
    pl.when(at_ref[2] == 0)(lambda: gather_into(layout, lambda cols: far[:, cols], blocks, capacity, width))


def backward_rows_kernel(early, experts, capacity, at_ref, ids, near, weight, steer, far, *refs):
    swapped, out = refs[: len(early)], refs[len(early) :]
    blocks, width = dict(enumerate(out)), near.shape[1]
    layout = slots_by_tokens(ids[...], at_ref[0], experts, capacity)

    @pl.when(at_ref[1] == 1)
    def _():
        others = {k: ref for k, ref in blocks.items() if k not in early}
        gather_into(layout, sent_at(near, weight, steer), others, capacity, width)
        for k, ref in zip(early, swapped):
            blocks[k][...] = ref[...]

    @pl.when(at_ref[1] == 0)
    def _():
        gather_into(layout, sent_at(far, weight, steer), blocks, capacity, width)


def hidden_kernel(count, *refs):
    rows, weights = refs[:count], refs[count : count + 4]
    own, other, x = refs[count + 4 :]
    x[...] = stacked([ref[...] for ref in rows])
    half, size = own.shape[0], weights[0].shape[1]
    for j in range(CORES):
        value = jax.nn.silu(dot(x[...], weights[j][...])) * dot(x[...], weights[CORES + j][...])
        cols = slice(j * size, (j + 1) * size)
        own[:, cols], other[:, cols] = value[:half].astype(BF16), value[half:].astype(BF16)


def out_kernel(capacity, own, other, d0, d1, *refs):
    d2, d3, out = refs[0], refs[1 : 1 + DOWN_PARTS], refs[1 + DOWN_PARTS :]
    size = d0.shape[0]
    for cols in pieces(d0.shape[1]):
        rows = dot(own[:, :size], d0[:, cols]) + dot(own[:, size:], d1[:, cols])
        rows = rows + dot(other[:, :size], d2[:, cols])
        rows = rows + dot(other[:, size:], stacked([ref[:, cols] for ref in d3]))
        for i, ref in enumerate(out):
            ref[:, cols] = rows[i * capacity : (i + 1) * capacity].astype(BF16)


def grad_hidden_kernel(*refs):
    rows, downs, (own, other, x) = refs[: -6 - DOWN_PARTS], refs[-6 - DOWN_PARTS : -3], refs[-3:]
    x[...] = stacked([ref[...] for ref in rows])
    size = downs[0].shape[0]
    groups = (downs[2:3], downs[3:], downs[:1], downs[1:2])
    for j, group in enumerate(groups):
        grads = dot_rows(x[...], stacked([ref[...] for ref in group]))
        ref = other if j < 2 else own
        ref[:, (j % 2) * size : (j % 2 + 1) * size] = grads.astype(ref.dtype)


def grad_rows_kernel(capacity, order, side, grads, kept, got, g0, g1, u0, u1, *refs):
    out, (gate_grad, up_grad) = refs[:-2], refs[-2:]
    size, height = g0.shape[1], grads.shape[0]
    here = slice(side * height, (side + 1) * height)
    for j, saved in enumerate((kept, got)):
        at = slice(j * size, (j + 1) * size)
        g, u = saved[here, :size].astype(F32), saved[here, size:].astype(F32)
        grad = grads[:, at].astype(F32)
        s = jax.nn.sigmoid(g)
        gate_grad[:, at] = (grad * u * s * (1.0 + g * (1.0 - s))).astype(BF16)
        up_grad[:, at] = (grad * g * s).astype(BF16)
    for cols in pieces(g0.shape[0]):
        rows = dot_rows(gate_grad[:, :size], g0[cols, :]) + dot_rows(gate_grad[:, size:], g1[cols, :])
        rows = rows + dot_rows(up_grad[:, :size], u0[cols, :]) + dot_rows(up_grad[:, size:], u1[cols, :])
        for ref, k in zip(out, order):
            ref[:, cols] = rows[k * capacity : (k + 1) * capacity].astype(ref.dtype)


def add_kernel(ours, theirs, out):
    out[...] = (ours[...] + theirs[...].astype(F32)).astype(BF16)


def forward_end_kernel(experts, capacity, at_ref, ids, near, far, weight, steer, *refs):
    back, (out, coefficient, mixed) = refs[:experts], refs[experts:]
    layout = tokens_by_slots(ids[...], at_ref[0], experts, capacity)
    unit = unit_of(steer[...])
    along, scale = 0.0, column(weight[...])
    for cols in pieces(near.shape[1]):
        rows = scale * dot(layout, stacked([ref[:, cols] for ref in back]))
        mixed[:, cols] = rows
        along = along + jnp.sum(rows * unit[:, cols], axis=1, keepdims=True)
    size = along.shape[0]
    diagonal = lax.broadcasted_iota(jnp.int32, (size, size), 0) == lax.broadcasted_iota(jnp.int32, (size, size), 1)
    coefficient[...] = jnp.sum(jnp.where(diagonal, along, 0.0), axis=0, keepdims=True)

    def finish(tokens):
        for cols in pieces(near.shape[1]):
            start = tokens[:, cols].astype(F32)
            out[:, cols] = (start + mixed[:, cols] - along * unit[:, cols]).astype(BF16)

    pl.when(at_ref[2] == 1)(lambda: finish(near))
    pl.when(at_ref[2] == 0)(lambda: finish(far))


def backward_most_kernel(ks, experts, capacity, at_ref, ids, near, far, *refs):
    back, out = dict(zip(ks, refs)), refs[-1]
    layout = tokens_by_slots(ids[...], at_ref[0], experts, capacity)

    def finish(tokens):
        for cols in pieces(near.shape[1]):
            empty = jnp.zeros((capacity, COLS), BF16)
            rows = dot(layout, stacked([back[k][:, cols] if k in back else empty for k in range(experts)]))
            out[:, cols] = (tokens[:, cols].astype(F32) + rows).astype(BF16)

    pl.when(at_ref[1] == 1)(lambda: finish(near))
    pl.when(at_ref[1] == 0)(lambda: finish(far))


def backward_end_kernel(k, experts, capacity, at_ref, ids, most, back, out):
    slot = slot_of(column(ids[...]), at_ref[0], experts, capacity, 0) - k * capacity
    wide = (slot.shape[0], capacity)
    layout = jnp.where(lax.broadcasted_iota(jnp.int32, wide, 1) == slot, 1.0, 0.0).astype(BF16)
    for cols in pieces(most.shape[1]):
        out[:, cols] = (most[:, cols].astype(F32) + dot(layout, back[:, cols])).astype(BF16)


def body(
    embedded,
    forward_held,
    forward_route,
    forward_weight,
    loss_cotangent,
    backward_held,
    backward_route,
    backward_weight,
    saved_gate,
    saved_up,
    gate_weight,
    up_weight,
    down_weight,
    steering,
):
    section_count = lax.axis_size("section")
    section_index = lax.axis_index("section")
    device_count = lax.axis_size("expert")
    device_index = lax.axis_index("expert")
    local_hidden = gate_weight.shape[2]
    holders = H // local_hidden
    experts = device_count // holders
    capacity = saved_gate.shape[1] // device_count
    rows = experts * capacity
    tokens, width = embedded.shape
    plane = device_index // holders
    chip = lax.rem(device_index, holders) // CORES
    core = lax.rem(device_index, CORES)
    first, last = section_index == 0, section_index == section_count - 1
    at = jnp.stack([plane, last.astype(jnp.int32), first.astype(jnp.int32), chip, core])
    early = [k for k in EARLY if k < experts]
    routed = [k for k in range(1, experts) if k not in early]

    def to_plane(value, by):
        pairs = [(i, (i + by * holders) % device_count) for i in range(device_count)]
        return lax.ppermute(value, "expert", pairs)

    def to_chip(value):
        pairs = [(i, i // holders * holders + (i + CORES) % holders) for i in range(device_count)]
        return lax.ppermute(value, "expert", pairs)

    def to_core(value):
        return lax.ppermute(value, "expert", [(i, i ^ 1) for i in range(device_count)])

    z_order, x_order = [], []

    def z_send(block, by, *deps, ahead=3):
        out = to_plane(after(block, *z_order[-ahead:][: len(z_order) >= ahead], *deps), by)
        z_order.append(out)
        return out

    def x_send(block):
        out = to_chip(after(block, *x_order[-2:][: len(x_order) >= 2]))
        x_order.append(out)
        return out

    gate, up, down = gate_weight[0], up_weight[0], down_weight[0]
    f_ids, b_ids = forward_route[0].reshape(1, tokens), backward_route[0].reshape(1, tokens)

    arriving = shifted(forward_held, "section", 1)[0]
    returning = shifted(backward_held, "section", -1)[0]
    d2 = to_chip(down)
    gate_sib, up_sib = to_core(gate), to_core(up)

    if section_count == 2:
        near_forward, near_backward = embedded, loss_cotangent
    else:
        near_forward = jnp.where(first, embedded, arriving)
        near_backward = jnp.where(last, loss_cotangent, returning)
    ones = call(
        functools.partial(first_kernel, early, experts, capacity),
        "first_rows",
        [shape(capacity, width)] * len(early),
        (at, f_ids, b_ids, near_forward, near_backward, backward_weight, steering),
        in_specs=[SMEM] + [VMEM] * 6,
        limit=56,
    )
    got_one = {k: z_send(block, k, gate_sib, up_sib) for k, block in zip(early, ones)}
    d1 = to_core(down)
    forward_rows = call(
        functools.partial(forward_rows_kernel, experts, capacity),
        "forward_rows",
        [shape(capacity, width)] * experts,
        (after(at, gate_sib, up_sib, d1), f_ids, embedded, arriving),
        in_specs=[SMEM] + [VMEM] * 3,
    )
    backward_rows = call(
        functools.partial(backward_rows_kernel, early, experts, capacity),
        "backward_rows",
        [shape(capacity, width)] * experts,
        (at, b_ids, loss_cotangent, backward_weight, steering, returning, *(forward_rows[k] for k in early)),
        in_specs=[SMEM] + [VMEM] * (5 + len(early)),
    )
    forward_got, backward_got = {0: forward_rows[0]}, {0: backward_rows[0]}
    for k in routed:
        forward_got[k] = z_send(forward_rows[k], k)
    got_two = {k: z_send(backward_rows[k], k) for k in early}

    kept, leaving = call(
        functools.partial(saved_kernel, experts, capacity),
        "saved_rows",
        [shape(CORES * rows, 2 * local_hidden)] * 2,
        (at, after(saved_gate[0], backward_rows[0]), saved_up[0]),
        in_specs=[SMEM] + [VMEM] * 2,
    )
    got = to_core(leaving)
    held = after(d2, *(forward_got[k] for k in routed))
    height = local_hidden // DOWN_PARTS
    d3 = [to_core(held[p * height : (p + 1) * height]) for p in range(DOWN_PARTS)]

    across = {}
    for k in routed:
        across[k] = x_send(forward_got[k])
        backward_got[k] = z_send(backward_rows[k], k, ahead=1)
    for k in early:
        forward_got[k] = jnp.where(last, got_two[k], got_one[k])
        backward_got[k] = jnp.where(last, got_one[k], got_two[k])
        across[k] = x_send(forward_got[k])
    across[0] = x_send(forward_got[0])
    columns_of = (gate, gate_sib, up, up_sib)
    downs = (down, d1, d2, *d3)

    forward_back, outs = {}, []
    for group in [each for each in (routed, early + [0]) if each]:
        height = len(group) * capacity
        own, other = call(
            functools.partial(hidden_kernel, 2 * len(group)),
            "hidden",
            [shape(height, 2 * local_hidden)] * 2,
            [after(forward_got[group[0]], got)]
            + [forward_got[k] for k in group[1:]]
            + [across[k] for k in group]
            + list(columns_of),
            in_specs=[VMEM] * (2 * len(group) + 4),
            scratch=[pltpu.VMEM((2 * height, width), BF16)],
            limit=16,
        )
        blocks = call(
            functools.partial(out_kernel, capacity),
            "expert_out",
            [shape(capacity, width)] * len(group),
            (own, x_send(other), *downs),
            in_specs=[VMEM] * (2 + len(downs)),
            limit=16,
        )
        outs.append(blocks[0])
        for k, block in zip(group, blocks):
            forward_back[k] = block if k == 0 else z_send(block, -k)

    grads_own, grads_other = call(
        grad_hidden_kernel,
        "grad_hidden",
        [shape(rows, 2 * local_hidden, F32), shape(rows, 2 * local_hidden)],
        [after(backward_got[0], outs[0])] + [backward_got[k] for k in range(1, experts)] + list(downs),
        in_specs=[VMEM] * (experts + len(downs)),
        scratch=[pltpu.VMEM((rows, width), BF16)],
        limit=16,
    )
    grads_got = x_send(grads_other)

    def grad_rows(grads, side, order, dtype):
        return call(
            functools.partial(grad_rows_kernel, capacity, order, side),
            "grad_rows",
            [shape(capacity, width, dtype)] * experts,
            (grads, kept, got, *columns_of),
            in_specs=[VMEM] * 7,
            scratch=[pltpu.VMEM((rows, 2 * local_hidden), BF16)] * 2,
            limit=16,
        )

    mine = grad_rows(grads_own, 0, list(range(experts)), F32)
    order = [k for k in RETURN_ORDER if k < experts]
    order += [k for k in range(experts) if k not in order]
    theirs = grad_rows(grads_got, 1, order, BF16)
    backward_back = {}
    for k, part in zip(order, theirs):
        block = call(add_kernel, "add_rows", [shape(capacity, width)], (mine[k], x_send(part)), in_specs=[VMEM] * 2)[0]
        backward_back[k] = block if k == 0 else z_send(block, -k)

    forward_out, coefficient = call(
        functools.partial(forward_end_kernel, experts, capacity),
        "forward_end",
        [shape(tokens, width), shape(1, tokens, F32)],
        (at, f_ids, embedded, arriving, forward_weight, steering, *(forward_back[k] for k in range(experts))),
        in_specs=[SMEM] + [VMEM] * (5 + experts),
        scratch=[pltpu.VMEM((tokens, width), F32)],
    )
    final = [k for k in order if k][-1]
    ks = [k for k in range(experts) if k != final]
    backward_most = call(
        functools.partial(backward_most_kernel, ks, experts, capacity),
        "backward_most",
        [shape(tokens, width)],
        (at, b_ids, loss_cotangent, returning, *(backward_back[k] for k in ks)),
        in_specs=[SMEM] + [VMEM] * (3 + len(ks)),
    )[0]
    backward_out = call(
        functools.partial(backward_end_kernel, final, experts, capacity),
        "backward_end",
        [shape(tokens, width)],
        (at, b_ids, backward_most, backward_back[final]),
        in_specs=[SMEM] + [VMEM] * 3,
    )[0]
    return (forward_out[None], coefficient, backward_out[None])


def solution(mesh):
    in_specs = (
        P("expert", None),
        P("section", "expert", None),
        P("section", "expert", None),
        P("section", "expert"),
        P("expert", None),
        P("section", "expert", None),
        P("section", "expert", None),
        P("section", "expert"),
        P("section", None, "expert"),
        P("section", None, "expert"),
        P("section", None, "expert"),
        P("section", None, "expert"),
        P("section", "expert", None),
        P("section", None),
    )
    out_specs = (P("section", "expert", None), P("section", "expert"), P("section", "expert", None))
    return jax.shard_map(body, mesh=mesh, in_specs=in_specs, out_specs=out_specs, check_vma=False)
```

```python
import functools

import jax
import jax.numpy as jnp
from jax import lax
from jax.experimental import pallas as pl
from jax.experimental.pallas import tpu as pltpu
from jax.sharding import PartitionSpec as P

H = 1024
CORES = 2
EARLY = (2,)
DOWN_PARTS = 2
RETURN_ORDER = (2, 1, 3, 0)
FLOPS = {"backward_most": 1000000, "grad_rows": 10000000000, "add_rows": 2000000000, "forward_end": 50000000000}
BF16 = jnp.bfloat16
F32 = jnp.float32
COLS = 896
ROWS_BY_ROWS = (((1,), (1,)), ((), ()))
SMEM = pl.BlockSpec(memory_space=pltpu.SMEM)
VMEM = pl.BlockSpec(memory_space=pltpu.VMEM)


def after(value, *deps):
    return lax.optimization_barrier((value, *deps))[0] if deps else value


def dot(a, b):
    return jnp.dot(a, b, preferred_element_type=F32)


def dot_rows(a, b):
    return lax.dot_general(a, b, ROWS_BY_ROWS, preferred_element_type=F32)


def shape(rows, cols, dtype=BF16):
    return jax.ShapeDtypeStruct((rows, cols), dtype)


def shifted(value, axis, by):
    devices = lax.axis_size(axis)
    pairs = [(i, i + by) for i in range(devices) if 0 <= i + by < devices]
    return lax.ppermute(value, axis, pairs)


def call(kernel, name, outs, args, grid=None, in_specs=None, out_specs=None, scratch=(), limit=24):
    extra = {} if grid is None else {"grid": grid}
    return pl.pallas_call(
        kernel,
        out_shape=outs,
        in_specs=in_specs,
        out_specs=out_specs if out_specs is not None else [VMEM] * len(outs),
        scratch_shapes=list(scratch),
        name=name,
        cost_estimate=pl.CostEstimate(flops=FLOPS.get(name, 5000000000), bytes_accessed=100000, transcendentals=0),
        compiler_params=pltpu.CompilerParams(vmem_limit_bytes=limit << 20),
        **extra,
    )(*args)


def stacked(values):
    if values[0].shape[0] % 16 == 0:
        return jnp.concatenate(values, axis=0)
    return jnp.concatenate([value.astype(F32) for value in values], axis=0).astype(BF16)


def slot_of(ids, plane, experts, capacity, axis):
    tokens = ids.shape[axis]
    wide = (tokens, 128) if axis == 0 else (max(8, experts), tokens)
    chosen = jnp.where(ids == lax.broadcasted_iota(jnp.int32, wide, 1 - axis), 1.0, 0.0)
    row = lax.broadcasted_iota(jnp.int32, (tokens, tokens), 0)
    col = lax.broadcasted_iota(jnp.int32, (tokens, tokens), 1)
    if axis == 0:
        earlier = dot(jnp.where(col < row, 1.0, 0.0).astype(BF16), chosen.astype(BF16))
    else:
        earlier = dot(chosen.astype(BF16), jnp.where(row < col, 1.0, 0.0).astype(BF16))
    position = jnp.sum(chosen * earlier, axis=1 - axis, keepdims=True).astype(jnp.int32)
    ahead = ids - plane
    return jnp.where(ahead < 0, ahead + experts, ahead) * capacity + position


def slots_by_tokens(ids_row, plane, experts, capacity):
    wide = (experts * capacity, ids_row.shape[1])
    slot = slot_of(ids_row, plane, experts, capacity, 1)
    return jnp.where(lax.broadcasted_iota(jnp.int32, wide, 0) == slot, 1.0, 0.0).astype(BF16)


def tokens_by_slots(ids_row, plane, experts, capacity):
    wide = (ids_row.shape[1], experts * capacity)
    slot = slot_of(column(ids_row), plane, experts, capacity, 0)
    return jnp.where(lax.broadcasted_iota(jnp.int32, wide, 1) == slot, 1.0, 0.0).astype(BF16)


def column(row):
    size = row.shape[1]
    diagonal = lax.broadcasted_iota(jnp.int32, (size, size), 0) == lax.broadcasted_iota(jnp.int32, (size, size), 1)
    return jnp.sum(jnp.where(diagonal, row, jnp.zeros_like(row)), axis=1, keepdims=True)


def unit_of(steer):
    return steer / jnp.sqrt(jnp.sum(steer * steer, axis=1, keepdims=True) + 1e-06)


def pieces(width):
    return [slice(at, at + COLS) for at in range(0, width, COLS)]


def gather_into(layout, tokens_at, blocks, capacity, width):
    for cols in pieces(width):
        rows = dot(layout, tokens_at(cols))
        for k, ref in blocks.items():
            ref[:, cols] = rows[k * capacity : (k + 1) * capacity].astype(BF16)


def sent_at(token_ref, weight_ref, steer_ref):
    unit = unit_of(steer_ref[...])

    def wide(cols):
        return token_ref[:, cols].astype(F32)

    along = 0.0
    for cols in pieces(unit.shape[1]):
        along = along + jnp.sum(wide(cols) * unit[:, cols], axis=1, keepdims=True)
    weight = column(weight_ref[...])
    return lambda cols: (weight * (wide(cols) - along * unit[:, cols])).astype(BF16)


def saved_kernel(experts, capacity, at_ref, saved_gate, saved_up, kept, leaving):
    plane, chip, core = at_ref[0], at_ref[3], at_ref[4]
    size = saved_gate.shape[1]
    wide = (capacity, saved_gate.shape[0])
    ahead = lax.broadcasted_iota(jnp.int32, wide, 1) - lax.broadcasted_iota(jnp.int32, wide, 0)
    for ref, core_index in ((kept, core), (leaving, 1 - core)):
        chosen = []
        for chip_index in (chip, 1 - chip):
            for k in range(experts):
                source = jnp.where(plane < k, plane - k + experts, plane - k)
                start = ((source * 2 + chip_index) * CORES + core_index) * capacity
                chosen.append(jnp.where(ahead == start, 1.0, 0.0))
        chosen = jnp.concatenate(chosen, axis=0).astype(BF16)
        ref[:, :size] = dot(chosen, saved_gate[...]).astype(BF16)
        ref[:, size:] = dot(chosen, saved_up[...]).astype(BF16)


def first_kernel(ks, experts, capacity, at_ref, f_ids, b_ids, f_tok, b_tok, b_weight, steer, *out):
    blocks, width = dict(zip(ks, out)), f_tok.shape[1]

    @pl.when(at_ref[1] == 1)
    def _():
        layout = slots_by_tokens(b_ids[...], at_ref[0], experts, capacity)
        gather_into(layout, sent_at(b_tok, b_weight, steer), blocks, capacity, width)

    @pl.when(at_ref[1] == 0)
    def _():
        layout = slots_by_tokens(f_ids[...], at_ref[0], experts, capacity)
        gather_into(layout, lambda cols: f_tok[:, cols], blocks, capacity, width)


def forward_rows_kernel(experts, capacity, at_ref, ids, near, far, *out):
    blocks, width = dict(enumerate(out)), near.shape[1]
    layout = slots_by_tokens(ids[...], at_ref[0], experts, capacity)
    pl.when(at_ref[2] == 1)(lambda: gather_into(layout, lambda cols: near[:, cols], blocks, capacity, width))
    pl.when(at_ref[2] == 0)(lambda: gather_into(layout, lambda cols: far[:, cols], blocks, capacity, width))


def backward_rows_kernel(early, experts, capacity, at_ref, ids, near, weight, steer, far, *refs):
    swapped, out = refs[: len(early)], refs[len(early) :]
    blocks, width = dict(enumerate(out)), near.shape[1]
    layout = slots_by_tokens(ids[...], at_ref[0], experts, capacity)

    @pl.when(at_ref[1] == 1)
    def _():
        others = {k: ref for k, ref in blocks.items() if k not in early}
        gather_into(layout, sent_at(near, weight, steer), others, capacity, width)
        for k, ref in zip(early, swapped):
            blocks[k][...] = ref[...]

    @pl.when(at_ref[1] == 0)
    def _():
        gather_into(layout, sent_at(far, weight, steer), blocks, capacity, width)


def hidden_kernel(count, *refs):
    rows, weights = refs[:count], refs[count : count + 4]
    own, other, x = refs[count + 4 :]
    x[...] = stacked([ref[...] for ref in rows])
    half, size = own.shape[0], weights[0].shape[1]
    for j in range(CORES):
        value = jax.nn.silu(dot(x[...], weights[j][...])) * dot(x[...], weights[CORES + j][...])
        cols = slice(j * size, (j + 1) * size)
        own[:, cols], other[:, cols] = value[:half].astype(BF16), value[half:].astype(BF16)


def out_kernel(capacity, own, other, d0, d1, *refs):
    d2, d3, out = refs[0], refs[1 : 1 + DOWN_PARTS], refs[1 + DOWN_PARTS :]
    size = d0.shape[0]
    for cols in pieces(d0.shape[1]):
        rows = dot(own[:, :size], d0[:, cols]) + dot(own[:, size:], d1[:, cols])
        rows = rows + dot(other[:, :size], d2[:, cols])
        rows = rows + dot(other[:, size:], stacked([ref[:, cols] for ref in d3]))
        for i, ref in enumerate(out):
            ref[:, cols] = rows[i * capacity : (i + 1) * capacity].astype(BF16)


def grad_hidden_kernel(*refs):
    rows, downs, (own, other, x) = refs[: -6 - DOWN_PARTS], refs[-6 - DOWN_PARTS : -3], refs[-3:]
    x[...] = stacked([ref[...] for ref in rows])
    size = downs[0].shape[0]
    groups = (downs[2:3], downs[3:], downs[:1], downs[1:2])
    for j, group in enumerate(groups):
        grads = dot_rows(x[...], stacked([ref[...] for ref in group]))
        ref = other if j < 2 else own
        ref[:, (j % 2) * size : (j % 2 + 1) * size] = grads.astype(ref.dtype)


def grad_rows_kernel(capacity, order, side, grads, kept, got, g0, g1, u0, u1, *refs):
    out, (gate_grad, up_grad) = refs[:-2], refs[-2:]
    size, height = g0.shape[1], grads.shape[0]
    here = slice(side * height, (side + 1) * height)
    for j, saved in enumerate((kept, got)):
        at = slice(j * size, (j + 1) * size)
        g, u = saved[here, :size].astype(F32), saved[here, size:].astype(F32)
        grad = grads[:, at].astype(F32)
        s = jax.nn.sigmoid(g)
        gate_grad[:, at] = (grad * u * s * (1.0 + g * (1.0 - s))).astype(BF16)
        up_grad[:, at] = (grad * g * s).astype(BF16)
    for cols in pieces(g0.shape[0]):
        rows = dot_rows(gate_grad[:, :size], g0[cols, :]) + dot_rows(gate_grad[:, size:], g1[cols, :])
        rows = rows + dot_rows(up_grad[:, :size], u0[cols, :]) + dot_rows(up_grad[:, size:], u1[cols, :])
        for ref, k in zip(out, order):
            ref[:, cols] = rows[k * capacity : (k + 1) * capacity].astype(ref.dtype)


def add_kernel(ours, theirs, out):
    out[...] = (ours[...] + theirs[...].astype(F32)).astype(BF16)


def forward_end_kernel(experts, capacity, at_ref, ids, near, far, weight, steer, *refs):
    back, (out, coefficient, mixed) = refs[:experts], refs[experts:]
    layout = tokens_by_slots(ids[...], at_ref[0], experts, capacity)
    unit = unit_of(steer[...])
    along, scale = 0.0, column(weight[...])
    for cols in pieces(near.shape[1]):
        rows = scale * dot(layout, stacked([ref[:, cols] for ref in back]))
        mixed[:, cols] = rows
        along = along + jnp.sum(rows * unit[:, cols], axis=1, keepdims=True)
    size = along.shape[0]
    diagonal = lax.broadcasted_iota(jnp.int32, (size, size), 0) == lax.broadcasted_iota(jnp.int32, (size, size), 1)
    coefficient[...] = jnp.sum(jnp.where(diagonal, along, 0.0), axis=0, keepdims=True)

    def finish(tokens):
        for cols in pieces(near.shape[1]):
            start = tokens[:, cols].astype(F32)
            out[:, cols] = (start + mixed[:, cols] - along * unit[:, cols]).astype(BF16)

    pl.when(at_ref[2] == 1)(lambda: finish(near))
    pl.when(at_ref[2] == 0)(lambda: finish(far))


def backward_most_kernel(ks, experts, capacity, at_ref, ids, near, far, *refs):
    back, out = dict(zip(ks, refs)), refs[-1]
    layout = tokens_by_slots(ids[...], at_ref[0], experts, capacity)

    def finish(tokens):
        for cols in pieces(near.shape[1]):
            empty = jnp.zeros((capacity, COLS), BF16)
            rows = dot(layout, stacked([back[k][:, cols] if k in back else empty for k in range(experts)]))
            out[:, cols] = (tokens[:, cols].astype(F32) + rows).astype(BF16)

    pl.when(at_ref[1] == 1)(lambda: finish(near))
    pl.when(at_ref[1] == 0)(lambda: finish(far))


def backward_end_kernel(k, experts, capacity, at_ref, ids, most, back, out):
    slot = slot_of(column(ids[...]), at_ref[0], experts, capacity, 0) - k * capacity
    wide = (slot.shape[0], capacity)
    layout = jnp.where(lax.broadcasted_iota(jnp.int32, wide, 1) == slot, 1.0, 0.0).astype(BF16)
    for cols in pieces(most.shape[1]):
        out[:, cols] = (most[:, cols].astype(F32) + dot(layout, back[:, cols])).astype(BF16)


def body(
    embedded,
    forward_held,
    forward_route,
    forward_weight,
    loss_cotangent,
    backward_held,
    backward_route,
    backward_weight,
    saved_gate,
    saved_up,
    gate_weight,
    up_weight,
    down_weight,
    steering,
):
    section_count = lax.axis_size("section")
    section_index = lax.axis_index("section")
    device_count = lax.axis_size("expert")
    device_index = lax.axis_index("expert")
    local_hidden = gate_weight.shape[2]
    holders = H // local_hidden
    experts = device_count // holders
    capacity = saved_gate.shape[1] // device_count
    rows = experts * capacity
    tokens, width = embedded.shape
    plane = device_index // holders
    chip = lax.rem(device_index, holders) // CORES
    core = lax.rem(device_index, CORES)
    first, last = section_index == 0, section_index == section_count - 1
    at = jnp.stack([plane, last.astype(jnp.int32), first.astype(jnp.int32), chip, core])
    early = [k for k in EARLY if k < experts]
    routed = [k for k in range(1, experts) if k not in early]

    def to_plane(value, by):
        pairs = [(i, (i + by * holders) % device_count) for i in range(device_count)]
        return lax.ppermute(value, "expert", pairs)

    def to_chip(value):
        pairs = [(i, i // holders * holders + (i + CORES) % holders) for i in range(device_count)]
        return lax.ppermute(value, "expert", pairs)

    def to_core(value):
        return lax.ppermute(value, "expert", [(i, i ^ 1) for i in range(device_count)])

    z_order, x_order = [], []

    def z_send(block, by, *deps, ahead=3):
        out = to_plane(after(block, *z_order[-ahead:][: len(z_order) >= ahead], *deps), by)
        z_order.append(out)
        return out

    def x_send(block):
        out = to_chip(after(block, *x_order[-2:][: len(x_order) >= 2]))
        x_order.append(out)
        return out

    gate, up, down = gate_weight[0], up_weight[0], down_weight[0]
    f_ids, b_ids = forward_route[0].reshape(1, tokens), backward_route[0].reshape(1, tokens)

    arriving = shifted(forward_held, "section", 1)[0]
    returning = shifted(backward_held, "section", -1)[0]
    d2 = to_chip(down)
    gate_sib, up_sib = to_core(gate), to_core(up)

    if section_count == 2:
        near_forward, near_backward = embedded, loss_cotangent
    else:
        near_forward = jnp.where(first, embedded, arriving)
        near_backward = jnp.where(last, loss_cotangent, returning)
    ones = call(
        functools.partial(first_kernel, early, experts, capacity),
        "first_rows",
        [shape(capacity, width)] * len(early),
        (at, f_ids, b_ids, near_forward, near_backward, backward_weight, steering),
        in_specs=[SMEM] + [VMEM] * 6,
        limit=56,
    )
    got_one = {k: z_send(block, k, gate_sib, up_sib) for k, block in zip(early, ones)}
    d1 = to_core(down)
    forward_rows = call(
        functools.partial(forward_rows_kernel, experts, capacity),
        "forward_rows",
        [shape(capacity, width)] * experts,
        (after(at, gate_sib, up_sib, d1), f_ids, embedded, arriving),
        in_specs=[SMEM] + [VMEM] * 3,
    )
    backward_rows = call(
        functools.partial(backward_rows_kernel, early, experts, capacity),
        "backward_rows",
        [shape(capacity, width)] * experts,
        (at, b_ids, loss_cotangent, backward_weight, steering, returning, *(forward_rows[k] for k in early)),
        in_specs=[SMEM] + [VMEM] * (5 + len(early)),
    )
    forward_got, backward_got = {0: forward_rows[0]}, {0: backward_rows[0]}
    for k in routed:
        forward_got[k] = z_send(forward_rows[k], k)
    got_two = {k: z_send(backward_rows[k], k) for k in early}

    kept, leaving = call(
        functools.partial(saved_kernel, experts, capacity),
        "saved_rows",
        [shape(CORES * rows, 2 * local_hidden)] * 2,
        (at, after(saved_gate[0], backward_rows[0]), saved_up[0]),
        in_specs=[SMEM] + [VMEM] * 2,
    )
    got = to_core(leaving)
    held = after(d2, *(forward_got[k] for k in routed))
    height = local_hidden // DOWN_PARTS
    d3 = [to_core(held[p * height : (p + 1) * height]) for p in range(DOWN_PARTS)]

    across = {}
    for k in routed:
        across[k] = x_send(forward_got[k])
        backward_got[k] = z_send(backward_rows[k], k, ahead=1)
    for k in early:
        forward_got[k] = jnp.where(last, got_two[k], got_one[k])
        backward_got[k] = jnp.where(last, got_one[k], got_two[k])
        across[k] = x_send(forward_got[k])
    across[0] = x_send(forward_got[0])
    columns_of = (gate, gate_sib, up, up_sib)
    downs = (down, d1, d2, *d3)

    forward_back, outs = {}, []
    for group in [each for each in (routed, early + [0]) if each]:
        height = len(group) * capacity
        own, other = call(
            functools.partial(hidden_kernel, 2 * len(group)),
            "hidden",
            [shape(height, 2 * local_hidden)] * 2,
            [after(forward_got[group[0]], got)]
            + [forward_got[k] for k in group[1:]]
            + [across[k] for k in group]
            + list(columns_of),
            in_specs=[VMEM] * (2 * len(group) + 4),
            scratch=[pltpu.VMEM((2 * height, width), BF16)],
            limit=16,
        )
        blocks = call(
            functools.partial(out_kernel, capacity),
            "expert_out",
            [shape(capacity, width)] * len(group),
            (own, x_send(other), *downs),
            in_specs=[VMEM] * (2 + len(downs)),
            limit=16,
        )
        outs.append(blocks[0])
        for k, block in zip(group, blocks):
            forward_back[k] = block if k == 0 else z_send(block, -k)

    grads_own, grads_other = call(
        grad_hidden_kernel,
        "grad_hidden",
        [shape(rows, 2 * local_hidden, F32), shape(rows, 2 * local_hidden)],
        [after(backward_got[0], outs[0])] + [backward_got[k] for k in range(1, experts)] + list(downs),
        in_specs=[VMEM] * (experts + len(downs)),
        scratch=[pltpu.VMEM((rows, width), BF16)],
        limit=16,
    )
    grads_got = x_send(grads_other)

    def grad_rows(grads, side, order, dtype):
        return call(
            functools.partial(grad_rows_kernel, capacity, order, side),
            "grad_rows",
            [shape(capacity, width, dtype)] * experts,
            (grads, kept, got, *columns_of),
            in_specs=[VMEM] * 7,
            scratch=[pltpu.VMEM((rows, 2 * local_hidden), BF16)] * 2,
            limit=16,
        )

    mine = grad_rows(grads_own, 0, list(range(experts)), F32)
    order = [k for k in RETURN_ORDER if k < experts]
    order += [k for k in range(experts) if k not in order]
    theirs = grad_rows(grads_got, 1, order, BF16)
    backward_back = {}
    for k, part in zip(order, theirs):
        block = call(add_kernel, "add_rows", [shape(capacity, width)], (mine[k], x_send(part)), in_specs=[VMEM] * 2)[0]
        backward_back[k] = block if k == 0 else z_send(block, -k)

    forward_out, coefficient = call(
        functools.partial(forward_end_kernel, experts, capacity),
        "forward_end",
        [shape(tokens, width), shape(1, tokens, F32)],
        (at, f_ids, embedded, arriving, forward_weight, steering, *(forward_back[k] for k in range(experts))),
        in_specs=[SMEM] + [VMEM] * (5 + experts),
        scratch=[pltpu.VMEM((tokens, width), F32)],
    )
    final = [k for k in order if k][-1]
    ks = [k for k in range(experts) if k != final]
    backward_most = call(
        functools.partial(backward_most_kernel, ks, experts, capacity),
        "backward_most",
        [shape(tokens, width)],
        (at, b_ids, loss_cotangent, returning, *(backward_back[k] for k in ks)),
        in_specs=[SMEM] + [VMEM] * (3 + len(ks)),
    )[0]
    backward_out = call(
        functools.partial(backward_end_kernel, final, experts, capacity),
        "backward_end",
        [shape(tokens, width)],
        (at, b_ids, backward_most, backward_back[final]),
        in_specs=[SMEM] + [VMEM] * 3,
    )[0]
    return (forward_out[None], coefficient, backward_out[None])


def solution(mesh):
    in_specs = (
        P("expert", None),
        P("section", "expert", None),
        P("section", "expert", None),
        P("section", "expert"),
        P("expert", None),
        P("section", "expert", None),
        P("section", "expert", None),
        P("section", "expert"),
        P("section", None, "expert"),
        P("section", None, "expert"),
        P("section", None, "expert"),
        P("section", None, "expert"),
        P("section", "expert", None),
        P("section", None),
    )
    out_specs = (P("section", "expert", None), P("section", "expert"), P("section", "expert", None))
    return jax.shard_map(body, mesh=mesh, in_specs=in_specs, out_specs=out_specs, check_vma=False)
```
